256 devices in a mesh: dp: 8 (over z), seq: 8 (over x_hi, y), tp: 4 (over x_lo, core).
Axes of the slice: x: 4 (x_hi: 2, x_lo: 2; x = x_hi * 2 + x_lo), y: 4, z: 8, core: 2. Of those that a mesh axis runs over, the one named last changes fastest.
Arguments:
- latent_query: bfloat16 [8, 4096, 2048], P('dp', ('seq', 'tp')), may hold values from -26 to 26
- latent_key: bfloat16 [8, 4096, 2048], P('dp', ('seq', 'tp')), may hold values from -26 to 26
- latent_value: bfloat16 [8, 4096, 2048], P('dp', ('seq', 'tp')), may hold values from -6 to 6
- out_grad: bfloat16 [8, 4096, 2048], P('dp', ('seq', 'tp')), may hold values from -384 to 384
- query_hidden: bfloat16 [8, 64, 3584], P('dp'), may hold values from -6 to 6
- cond_weight: bfloat16 [3584, 2, 2048], P(None, None, 'seq'), may hold values from -0.09375 to 0.09375
Outputs:
- grad_query: bfloat16 [8, 4096, 2048], P('dp', ('seq', 'tp'))
- grad_key: bfloat16 [8, 4096, 2048], P('dp', ('seq', 'tp'))
- grad_value: bfloat16 [8, 4096, 2048], P('dp', ('seq', 'tp'))
- grad_cond_weight: float32 [3584, 2, 2048], P(('dp', 'tp'), None, 'seq')
The draws below stay inside these ranges and needn't reach their ends.
All inputs are finite; a program needn't handle non-finite values.
Results may differ from the reference program's by a relative error of at most 0.009.
Values may be sent and summed in bfloat16 or wider, within the bound.
A program may use at most 192 MiB of HBM per device.

```python
import jax
import jax.numpy as jnp
from jax import lax

HD = 128
HL = 3584
QUERIES = 64
HEADS = 16
FEAT = 2048
SEQ_LEN = 4096
SAMPLES = 8


def draw_latent_query(key, part):
    key = jax.random.fold_in(key, 5)
    values = jax.random.normal(key, (SAMPLES, SEQ_LEN, FEAT), jnp.float32)
    return values.astype(jnp.bfloat16)


def draw_latent_key(key, part):
    key = jax.random.fold_in(key, 9)
    values = jax.random.normal(key, (SAMPLES, SEQ_LEN, FEAT), jnp.float32)
    return values.astype(jnp.bfloat16)


def level_of(own_key, dims, pieces, low, largest):
    loudness = 1.0
    for dim, parts in pieces:
        heights = jax.random.uniform(jax.random.fold_in(jax.random.fold_in(own_key, 6), dim), (parts,), jnp.float32, low / len(pieces), largest / len(pieces))
        loudness = loudness * jnp.repeat(jnp.exp(heights), dims[dim] // parts).reshape((-1,) + (1,) * (len(dims) - 1 - dim))
    return loudness


def bell_draw(key, shape, width, limit, pieces=(), held_as=jnp.bfloat16):
    drawn = width * jax.random.normal(key, shape, jnp.float32)
    if pieces:
        drawn = drawn * level_of(key, shape, pieces, -0.22, 0.18)
    return jnp.clip(drawn, -limit, limit).astype(held_as)


def setup_inputs(seed: int = 0) -> dict:
    splits = jax.random.split(jax.random.key(seed), 7)
    latent_query = draw_latent_query(jax.random.fold_in(splits[6], 71), 0)
    latent_key = draw_latent_key(jax.random.fold_in(splits[6], 71), 0)
    latent_value = bell_draw(splits[2], (SAMPLES, SEQ_LEN, FEAT), 1.0, 6.0, ((0, 8), (1, 32)))
    out_grad = bell_draw(splits[3], (SAMPLES, SEQ_LEN, FEAT), 64.0, 384.0, ((0, 8), (1, 32)))
    query_hidden = bell_draw(splits[4], (SAMPLES, QUERIES, HL), 1.0, 6.0, ((0, 8),))
    cond_weight = bell_draw(splits[5], (HL, 2, FEAT), HL ** -0.5, 0.09375, ((2, 8),))
    return dict(latent_query=latent_query, latent_key=latent_key, latent_value=latent_value, out_grad=out_grad, query_hidden=query_hidden, cond_weight=cond_weight)


def per_sample(query_rows, key_rows, value_rows, grad_rows, hidden_rows, cond_weight):
    score_scale = HD ** -0.5
    cond = jnp.dot(hidden_rows, cond_weight.reshape(HL, 2 * FEAT), preferred_element_type=jnp.float32)
    cond = cond.astype(jnp.bfloat16).reshape(QUERIES, 2, FEAT)
    key_full = jnp.concatenate([key_rows, cond[:, 0]], 0)
    value_full = jnp.concatenate([value_rows, cond[:, 1]], 0)

    def per_head(index):
        offset = index * HD

        def column(matrix):
            return lax.dynamic_slice_in_dim(matrix, offset, HD, 1).astype(jnp.float32)

        query_part = column(query_rows)
        key_part = column(key_full)
        value_part = column(value_full)
        grad_part = column(grad_rows)
        scores = jnp.dot(query_part, key_part.T, precision=lax.Precision.HIGHEST) * score_scale
        row_max = jnp.max(scores, axis=1, keepdims=True)
        weights_exp = jnp.exp(scores - row_max)
        probs = weights_exp / jnp.sum(weights_exp, axis=1, keepdims=True)
        dprobs = jnp.dot(grad_part, value_part.T, precision=lax.Precision.HIGHEST)
        dot_sum = jnp.sum(probs * dprobs, axis=1, keepdims=True)
        dscores = lax.optimization_barrier((probs * (dprobs - dot_sum)).astype(jnp.bfloat16)).astype(jnp.float32)
        probs_low = lax.optimization_barrier(probs.astype(jnp.bfloat16)).astype(jnp.float32)
        grad_q = (jnp.dot(dscores, key_part, precision=lax.Precision.HIGHEST) * score_scale).astype(jnp.bfloat16)
        key_total = jnp.dot(dscores.T, query_part, precision=lax.Precision.HIGHEST) * score_scale
        value_total = jnp.dot(probs_low.T, grad_part, precision=lax.Precision.HIGHEST)
        return grad_q, key_total, value_total

    grad_q, key_total, value_total = lax.map(per_head, jnp.arange(HEADS, dtype=jnp.int32))
    grad_query = grad_q.transpose(1, 0, 2).reshape(SEQ_LEN, FEAT)
    key_total = key_total.transpose(1, 0, 2).reshape(SEQ_LEN + QUERIES, FEAT)
    value_total = value_total.transpose(1, 0, 2).reshape(SEQ_LEN + QUERIES, FEAT)
    grad_key = key_total[:SEQ_LEN].astype(jnp.bfloat16)
    grad_value = value_total[:SEQ_LEN].astype(jnp.bfloat16)
    cond_grad = jnp.stack([key_total[SEQ_LEN:], value_total[SEQ_LEN:]], 1).reshape(QUERIES, 2 * FEAT)
    weight_term = jnp.dot(hidden_rows.astype(jnp.float32).T, cond_grad, precision=lax.Precision.HIGHEST)
    return grad_query, grad_key, grad_value, weight_term


def reference(latent_query, latent_key, latent_value, out_grad, query_hidden, cond_weight):
    def step_sample(total, inputs):
        query_rows, key_rows, value_rows, grad_rows, hidden_rows = inputs
        grad_query, grad_key, grad_value, weight_term = per_sample(query_rows, key_rows, value_rows, grad_rows, hidden_rows, cond_weight)
        return total + weight_term, (grad_query, grad_key, grad_value)

    start_total = jnp.zeros((HL, 2 * FEAT), jnp.float32)
    weight_total, grads = lax.scan(step_sample, start_total, (latent_query, latent_key, latent_value, out_grad, query_hidden))
    return grads[0], grads[1], grads[2], weight_total.reshape(HL, 2, FEAT)
```

```python
import jax
import jax.numpy as jnp
from jax import lax
from jax.experimental import pallas as pl
from jax.experimental.pallas import tpu as pltpu
from jax.sharding import PartitionSpec as P

HD = 128
MESH = pl.DeviceIdType.MESH
F32 = jnp.float32
BF16 = jnp.bfloat16
SCALE = HD ** (-0.5)
SCALE2 = SCALE * 1.4426950408889634
ROWS = 128
SLOTS = 16
QB = 1024
KT = 1024
KEYS = 4096
COND = 64
TILES = KEYS // KT
TILE_SLOTS = SLOTS // TILES
BLOCK_SLOTS = QB // ROWS
WINDOW = 512


def mm(a, b, ca, cb):
    return lax.dot_general(a, b, (((ca,), (cb,)), ((), ())), preferred_element_type=F32)


def gray(a):
    return a + (a // 2) * (1 - 2 * (a % 2))


def offset_of(slot):
    return gray(slot // 4), gray(slot % 4)


def rows_at(start, size):
    if isinstance(start, int):
        return pl.ds(start, size)
    return pl.ds(pl.multiple_of(start, 64), size)


def arrived(ref, sem):
    pltpu.make_async_copy(ref, ref, sem).wait()


def kernel(
    lq, lk, lv, og, hid, cw,
    dq_o, dk_o, dv_o, w_o,
    qb, gb, kb, vb, qt, gt, e_s, dp_s, m_s, ka, va, dqb,
    st, rx, fin, cwv, hida, c_st, c_rx, cga, prod,
    in_s, in_r, fw_s, fw_r, ex_s, ex_r, out_s, out_r,
    hid_s, hid_r, c1_s, c1_r, cg_s, cg_r, w_s, w_r, cw_sem,
):
    z = lax.axis_index("dp")
    seq = lax.axis_index("seq")
    tp = lax.axis_index("tp")
    x = (seq // 4) * 2 + tp // 2
    y = seq % 4
    core = tp % 2
    head = 2 * seq + tp // 2
    partner = {"tp": (tp // 2) * 2 + 1 - core}

    def chip(slot, sign):
        dx, dy = offset_of(slot)
        cx = (x + sign * dx + 4) % 4
        cy = (y + sign * dy + 4) % 4
        cseq = (cx // 2) * 4 + cy
        return {"seq": cseq, "tp": (cx % 2) * 2 + core}, 2 * cseq + cx % 2

    def feat(index):
        return pl.ds(pl.multiple_of(index * HD, HD), HD)

    barrier = pltpu.get_barrier_semaphore()

    def greet(slot, carry):
        device, _ = chip(slot, 1)
        pl.semaphore_signal(barrier, inc=1, device_id=device, device_id_type=MESH)
        return carry

    lax.fori_loop(1, SLOTS, greet, 0)
    pl.semaphore_signal(barrier, inc=1, device_id=partner, device_id_type=MESH)
    pl.semaphore_signal(barrier, inc=1, device_id={"tp": 3 - tp}, device_id_type=MESH)
    for dz in range(1, 8):
        pl.semaphore_signal(
            barrier, inc=1, device_id={"dp": (z + dz) % 8}, device_id_type=MESH
        )

    weights = pltpu.make_async_copy(
        cw.at[:, :, feat(tp // 2)], cwv, cw_sem
    )
    weights.start()
    for a, (src, dst) in enumerate(((lq, qb), (og, gb))):
        pltpu.make_async_copy(src.at[0, :, feat(head)], dst.at[pl.ds(0, ROWS)], in_r.at[a, 0]).start()
    for a, (src, dst) in enumerate(((lk, kb), (lv, vb))):
        pltpu.make_async_copy(
            src.at[0, :, feat(head)], dst.at[rows_at(core * ROWS, ROWS)], in_r.at[2 + a, 0]
        ).start()

    pl.semaphore_wait(barrier, 24)

    def in_copy(a, src, dst, dst_start, slot):
        device, there = chip(slot, 1)
        return pltpu.make_async_remote_copy(
            src_ref=src.at[0, :, feat(there)],
            dst_ref=dst.at[rows_at(dst_start, ROWS)],
            send_sem=in_s.at[a, slot],
            recv_sem=in_r.at[a, slot],
            device_id=device,
            device_id_type=MESH,
        )

    def send_q(slot, carry):
        in_copy(0, lq, qb, slot * ROWS, slot).start()
        in_copy(1, og, gb, slot * ROWS, slot).start()
        return carry

    def send_k(slot, carry):
        in_copy(2, lk, kb, slot * 2 * ROWS + core * ROWS, slot).start()
        in_copy(3, lv, vb, slot * 2 * ROWS + core * ROWS, slot).start()
        return carry

    lax.fori_loop(1, TILE_SLOTS, send_k, 0)
    lax.fori_loop(1, BLOCK_SLOTS, send_q, 0)
    lax.fori_loop(TILE_SLOTS, SLOTS, send_k, 0)
    lax.fori_loop(BLOCK_SLOTS, SLOTS, send_q, 0)

    def window(zz):
        return pl.ds(pl.multiple_of((7 * zz // 2) * HD, HD), WINDOW)

    for dz in range(1, 8):
        there = (z + dz) % 8
        pltpu.make_async_remote_copy(
            src_ref=hid.at[0, :, window(there)],
            dst_ref=hida.at[dz],
            send_sem=hid_s.at[dz],
            recv_sem=hid_r.at[dz],
            device_id={"dp": there},
            device_id_type=MESH,
        ).start()
    hida[0] = hid[0, :, window(z)]

    weights.wait()

    def cond_step(i, sums):
        r = pl.multiple_of(i * 512, 512)
        rows = hid[0, :, pl.ds(r, 512)]
        return (
            sums[0] + mm(rows, cwv[pl.ds(r, 512), 0, :], 1, 0),
            sums[1] + mm(rows, cwv[pl.ds(r, 512), 1, :], 1, 0),
        )

    nothing = jnp.zeros((COND, HD), F32)
    cond_k, cond_v = lax.fori_loop(0, 7, cond_step, (nothing, nothing))
    kb[pl.ds(KEYS, COND), :] = cond_k.astype(BF16)
    vb[pl.ds(KEYS, COND), :] = cond_v.astype(BF16)
    ka[...] = jnp.zeros_like(ka)
    va[...] = jnp.zeros_like(va)

    def take_queries(block):
        def wait_q(slot, carry):
            for a, dst in enumerate((qb, gb)):
                arrived(dst.at[rows_at(slot * ROWS, ROWS)], in_r.at[a, slot])
            return carry

        lax.fori_loop(block * BLOCK_SLOTS, (block + 1) * BLOCK_SLOTS, wait_q, 0)
        qt[...] = qb[pl.ds(block * QB, QB), :].T
        gt[...] = gb[pl.ds(block * QB, QB), :].T

    def take_keys(tile):
        def wait_k(i, carry):
            slot = tile * TILE_SLOTS + i
            for a, dst in enumerate((kb, vb)):
                mine = dst.at[rows_at(slot * 2 * ROWS + core * ROWS, ROWS)]
                arrived(mine, in_r.at[2 + a, slot])
                pltpu.make_async_remote_copy(
                    src_ref=mine,
                    dst_ref=mine,
                    send_sem=fw_s.at[a, slot],
                    recv_sem=fw_r.at[a, slot],
                    device_id=partner,
                    device_id_type=MESH,
                ).start()
            return carry

        def wait_f(i, carry):
            slot = tile * TILE_SLOTS + i
            for a, dst in enumerate((kb, vb)):
                arrived(dst.at[rows_at(slot * 2 * ROWS + (1 - core) * ROWS, ROWS)], fw_r.at[a, slot])
            return carry

        lax.fori_loop(0, TILE_SLOTS, wait_k, 0)
        lax.fori_loop(0, TILE_SLOTS, wait_f, 0)

    def forward(tile, stats, start, size):
        top, total, dots = stats
        keys = rows_at(start, size)
        scores = mm(kb[keys, :], qt[...], 1, 0)
        dprobs = mm(vb[keys, :], gt[...], 1, 0)
        top_new = jnp.maximum(top, jnp.max(scores, axis=0, keepdims=True) * SCALE2)
        e = jnp.exp2(scores * SCALE2 - top_new)
        shrink = jnp.exp2(top - top_new)
        total = total * shrink + jnp.sum(e, axis=0, keepdims=True)
        dots = dots * shrink + jnp.sum(e * dprobs, axis=0, keepdims=True)
        e_s[keys, :] = e.astype(BF16)
        dp_s[keys, :] = dprobs
        m_s[pl.ds(tile, 1), :] = top_new
        return top_new, total, dots

    def backward(tile, dq, stats, start, size):
        top, inverse, mean = stats
        keys = rows_at(start, size)
        factor = jnp.exp2(m_s[pl.ds(tile, 1), :] - top) * inverse
        grads = (gt[...].astype(F32) * factor).astype(BF16)
        queries = (qt[...].astype(F32) * (factor * SCALE)).astype(BF16)
        e = e_s[keys, :]
        ds = (e.astype(F32) * (dp_s[keys, :] - mean)).astype(BF16)
        va[keys, :] += mm(e, grads, 1, 1)
        ka[keys, :] += mm(ds, queries, 1, 1)
        return dq + mm(kb[keys, :], ds, 0, 0) * (factor * SCALE)

    def forward_all(block):
        low = jnp.full((1, QB), -1e30, F32)
        zero = jnp.zeros((1, QB), F32)

        def step(tile, stats):
            if block == 0:
                take_keys(tile)
            return forward(tile, stats, tile * KT, KT)

        stats = forward(TILES, (low, zero, zero), KEYS, COND)
        top, total, dots = lax.fori_loop(0, TILES, step, stats)
        inverse = 1.0 / total
        return top, inverse, dots * inverse

    def out_copy(a, src, dst, slot):
        device, _ = chip(slot, -1)
        return pltpu.make_async_remote_copy(
            src_ref=src,
            dst_ref=dst.at[0, :, feat(head)],
            send_sem=out_s.at[a, slot],
            recv_sem=out_r.at[a, slot],
            device_id=device,
            device_id_type=MESH,
        )

    def send_out(a, src, dst, slot):
        @pl.when(slot > 0)
        def _():
            out_copy(a, src, dst, slot).start()

        @pl.when(slot == 0)
        def _():
            pltpu.make_async_copy(src, dst.at[0, :, feat(head)], out_r.at[a, 0]).start()

    def send_dq(block, dq):
        dqb[pl.ds(block * QB, QB), :] = dq.T.astype(BF16)

        def one(slot, carry):
            send_out(0, dqb.at[rows_at(slot * ROWS, ROWS)], dq_o, slot)
            return carry

        lax.fori_loop(block * BLOCK_SLOTS, (block + 1) * BLOCK_SLOTS, one, 0)

    empty = jnp.zeros((HD, QB), F32)

    take_queries(0)
    stats = forward_all(0)
    dq = backward(TILES, empty, stats, KEYS, COND)
    dq = lax.fori_loop(0, TILES, lambda t, d: backward(t, d, stats, t * KT, KT), dq)
    send_dq(0, dq)

    take_queries(1)
    stats = forward_all(1)
    dq = backward(TILES, empty, stats, KEYS, COND)

    @pl.when(core == 0)
    def _():
        c_st[...] = va[pl.ds(KEYS, COND), :].astype(BF16)

    @pl.when(core == 1)
    def _():
        c_st[...] = ka[pl.ds(KEYS, COND), :].astype(BF16)

    pltpu.make_async_remote_copy(
        src_ref=c_st, dst_ref=c_rx, send_sem=c1_s, recv_sem=c1_r, device_id=partner, device_id_type=MESH
    ).start()

    def cond_sum():
        arrived(c_rx, c1_r)

        @pl.when(core == 0)
        def _():
            cga[0] = (ka[pl.ds(KEYS, COND), :] + c_rx[...].astype(F32)).astype(BF16)

        @pl.when(core == 1)
        def _():
            cga[0] = (va[pl.ds(KEYS, COND), :] + c_rx[...].astype(F32)).astype(BF16)

        for dz in range(1, 8):
            pltpu.make_async_remote_copy(
                src_ref=cga.at[0],
                dst_ref=cga.at[dz],
                send_sem=cg_s.at[dz],
                recv_sem=cg_r.at[dz],
                device_id={"dp": (z + dz) % 8},
                device_id_type=MESH,
            ).start()

    def part_copy(dt):
        owner = (tp + dt) % 4
        return pltpu.make_async_remote_copy(
            src_ref=prod.at[pl.ds(pl.multiple_of((z % 2) * 64 + owner * 112, 16), 112)],
            dst_ref=w_o.at[tp],
            send_sem=w_s.at[dt],
            recv_sem=w_r.at[dt],
            device_id={"tp": owner},
            device_id_type=MESH,
        )

    def cond_product():
        for dz in range(1, 8):
            arrived(hida.at[dz], hid_r.at[dz])
            arrived(cga.at[dz], cg_r.at[dz])
        prod[...] = mm(
            hida[...].reshape(8 * COND, WINDOW), cga[...].reshape(8 * COND, HD), 0, 0
        )
        for dt in range(1, 4):
            part_copy(dt).start()
        pltpu.make_async_copy(
            prod.at[pl.ds(pl.multiple_of((z % 2) * 64 + tp * 112, 16), 112)], w_o.at[tp], w_r.at[0]
        ).start()

    def tile_slots(tile):
        return pl.ds(pl.multiple_of(tile * TILE_SLOTS, TILE_SLOTS), TILE_SLOTS)

    def swap(tile):
        for i in range(TILE_SLOTS):
            slot = tile * TILE_SLOTS + i
            theirs = rows_at(slot * 2 * ROWS + (1 - core) * ROWS, ROWS)
            st[0, slot] = ka[theirs, :].astype(BF16)
            st[1, slot] = va[theirs, :].astype(BF16)
        for a in range(2):
            pltpu.make_async_remote_copy(
                src_ref=st.at[a, tile_slots(tile)],
                dst_ref=rx.at[a, tile_slots(tile)],
                send_sem=ex_s.at[a, tile],
                recv_sem=ex_r.at[a, tile],
                device_id=partner,
                device_id_type=MESH,
            ).start()

    def finish(tile):
        for a in range(2):
            arrived(rx.at[a, tile_slots(tile)], ex_r.at[a, tile])
        for i in range(TILE_SLOTS):
            slot = tile * TILE_SLOTS + i
            mine = rows_at(slot * 2 * ROWS + core * ROWS, ROWS)
            for a, (acc, dst) in enumerate(((ka, dk_o), (va, dv_o))):
                fin[a, slot] = (acc[mine, :] + rx[a, slot].astype(F32)).astype(BF16)
                send_out(1 + a, fin.at[a, slot], dst, slot)

    def last(i, d):
        tile = TILES - 1 - i
        d = backward(tile, d, stats, tile * KT, KT)
        swap(tile)

        @pl.when(i > 0)
        def _():
            finish(tile + 1)

        @pl.when(i == 0)
        def _():
            cond_sum()

        @pl.when(i == TILES - 2)
        def _():
            cond_product()

        return d

    dq = lax.fori_loop(0, TILES, last, dq)
    send_dq(1, dq)
    finish(0)

    def drain(slot, carry):
        for a, dst in enumerate((dq_o, dk_o, dv_o)):
            arrived(dst.at[0, :, feat(0)], out_r.at[a, slot])
        return carry

    def drain_sends(slot, carry):
        for a in range(4):
            arrived(qb.at[pl.ds(0, ROWS)], in_s.at[a, slot])
        for a in range(3):
            arrived(dqb.at[pl.ds(0, ROWS)], out_s.at[a, slot])
        return carry

    def drain_forwards(slot, carry):
        for a in range(2):
            arrived(kb.at[pl.ds(0, ROWS)], fw_s.at[a, slot])
        return carry

    lax.fori_loop(0, SLOTS, drain_forwards, 0)
    lax.fori_loop(1, SLOTS, drain_sends, 0)
    for tile in range(TILES):
        for a in range(2):
            arrived(st.at[a, pl.ds(tile * TILE_SLOTS, TILE_SLOTS)], ex_s.at[a, tile])
    arrived(c_st, c1_s)
    for dz in range(1, 8):
        arrived(hida.at[dz], hid_s.at[dz])
        arrived(cga.at[0], cg_s.at[dz])
    for dt in range(4):
        if dt:
            arrived(prod.at[pl.ds(0, 112)], w_s.at[dt])
        arrived(w_o.at[0], w_r.at[dt])
    lax.fori_loop(0, SLOTS, drain, 0)


def on_device(latent_query, latent_key, latent_value, out_grad, query_hidden, cond_weight):
    anywhere = pl.BlockSpec(memory_space=pl.ANY)
    token = jax.ShapeDtypeStruct(latent_query.shape, BF16)
    dma = pltpu.SemaphoreType.DMA
    total_keys = KEYS + COND
    grads = pl.pallas_call(
        kernel,
        name="attention_backward",
        out_shape=(token, token, token, jax.ShapeDtypeStruct((4, 112, HD), F32)),
        in_specs=[anywhere] * 4 + [pl.BlockSpec(memory_space=pltpu.VMEM), anywhere],
        out_specs=(anywhere,) * 4,
        scratch_shapes=[
            pltpu.VMEM((2 * QB, HD), BF16),
            pltpu.VMEM((2 * QB, HD), BF16),
            pltpu.VMEM((total_keys, HD), BF16),
            pltpu.VMEM((total_keys, HD), BF16),
            pltpu.VMEM((HD, QB), BF16),
            pltpu.VMEM((HD, QB), BF16),
            pltpu.VMEM((total_keys, QB), BF16),
            pltpu.VMEM((total_keys, QB), F32),
            pltpu.VMEM((8, QB), F32),
            pltpu.VMEM((total_keys, HD), F32),
            pltpu.VMEM((total_keys, HD), F32),
            pltpu.VMEM((2 * QB, HD), BF16),
            pltpu.VMEM((2, SLOTS, ROWS, HD), BF16),
            pltpu.VMEM((2, SLOTS, ROWS, HD), BF16),
            pltpu.VMEM((2, SLOTS, ROWS, HD), BF16),
            pltpu.VMEM((cond_weight.shape[0], 2, HD), BF16),
            pltpu.VMEM((8, COND, WINDOW), BF16),
            pltpu.VMEM((COND, HD), BF16),
            pltpu.VMEM((COND, HD), BF16),
            pltpu.VMEM((8, COND, HD), BF16),
            pltpu.VMEM((WINDOW, HD), F32),
            dma((4, SLOTS)), dma((4, SLOTS)),
            dma((2, SLOTS)), dma((2, SLOTS)),
            dma((2, TILES)), dma((2, TILES)),
            dma((3, SLOTS)), dma((3, SLOTS)),
            dma((8,)), dma((8,)),
            dma, dma,
            dma((8,)), dma((8,)),
            dma((4,)), dma((4,)),
            dma,
        ],
        compiler_params=pltpu.CompilerParams(
            collective_id=0, has_side_effects=True, vmem_limit_bytes=60 << 20
        ),
    )(latent_query, latent_key, latent_value, out_grad, query_hidden, cond_weight)
    out_query, out_key, out_value, parts = grads
    weight = parts.reshape(2, 2, 112, HD).transpose(2, 1, 0, 3).reshape(112, 2, 2 * HD)
    return (out_query, out_key, out_value, weight)


def solution(mesh):
    placed = (
        P("dp", ("seq", "tp"), None),
        P("dp", ("seq", "tp"), None),
        P("dp", ("seq", "tp"), None),
        P("dp", ("seq", "tp"), None),
        P("dp", None, None),
        P(None, None, "seq"),
    )
    return jax.shard_map(
        on_device,
        mesh=mesh,
        in_specs=placed,
        out_specs=(
            P("dp", ("seq", "tp"), None),
            P("dp", ("seq", "tp"), None),
            P("dp", ("seq", "tp"), None),
            P(("dp", "tp"), None, "seq"),
        ),
        check_vma=False,
    )
```

```python
import jax
import jax.numpy as jnp
from jax import lax
from jax.experimental import pallas as pl
from jax.experimental.pallas import tpu as pltpu
from jax.sharding import PartitionSpec as P

HD = 128
MESH = pl.DeviceIdType.MESH
F32 = jnp.float32
BF16 = jnp.bfloat16
SCALE = HD ** (-0.5)
SCALE2 = SCALE * 1.4426950408889634
ROWS = 128
SLOTS = 16
QB = 1024
KT = 512
BT = 2 * KT
KEYS = 4096
COND = 64
TILES = KEYS // KT
TILE_SLOTS = SLOTS // TILES
BACK_TILES = KEYS // BT
BACK_SLOTS = SLOTS // BACK_TILES
HALF_SLOTS = QB // ROWS
GROUP = 4
WINDOW = 512


def mm(a, b, ca, cb):
    return lax.dot_general(a, b, (((ca,), (cb,)), ((), ())), preferred_element_type=F32)


def offset_of(slot):
    return slot % 4, (slot % 4 + slot // 4) % 4


def rows_at(start, size):
    if isinstance(start, int):
        return pl.ds(start, size)
    return pl.ds(pl.multiple_of(start, 64), size)


def arrived(ref, sem):
    pltpu.make_async_copy(ref, ref, sem).wait()


def kernel(
    lq, lk, lv, og, hid, cw,
    dq_o, dk_o, dv_o, w_o,
    qb, gb, kb, vb, qt, gt, qi, gi, e_s, dp_s, m_s, ka, va, dqa, dqb,
    st, rx, fin, cwv, hida, c_st, c_rx, cga, prod,
    in_s, q_r, k_r, fw_s, fw_r, ex_s, ex_r, out_s, out_r,
    hid_s, hid_r, c1_s, c1_r, cg_s, cg_r, w_s, w_r, cw_sem,
):
    z = lax.axis_index("dp")
    seq = lax.axis_index("seq")
    tp = lax.axis_index("tp")
    x = (seq // 4) * 2 + tp // 2
    y = seq % 4
    core = tp % 2
    head = 2 * seq + tp // 2
    partner = {"tp": (tp // 2) * 2 + 1 - core}

    def chip(slot, sign):
        dx, dy = offset_of(slot)
        cx = (x + sign * dx + 4) % 4
        cy = (y + sign * dy + 4) % 4
        cseq = (cx // 2) * 4 + cy
        return {"seq": cseq, "tp": (cx % 2) * 2 + core}, 2 * cseq + cx % 2

    def feat(index):
        return pl.ds(pl.multiple_of(index * HD, HD), HD)

    barrier = pltpu.get_barrier_semaphore()

    def greet(slot, carry):
        device, _ = chip(slot, 1)
        pl.semaphore_signal(barrier, inc=1, device_id=device, device_id_type=MESH)
        return carry

    lax.fori_loop(1, SLOTS, greet, 0)
    pl.semaphore_signal(barrier, inc=1, device_id=partner, device_id_type=MESH)
    pl.semaphore_signal(barrier, inc=1, device_id={"tp": 3 - tp}, device_id_type=MESH)
    for dz in range(1, 8):
        pl.semaphore_signal(
            barrier, inc=1, device_id={"dp": (z + dz) % 8}, device_id_type=MESH
        )

    weights = pltpu.make_async_copy(
        cw.at[:, :, feat(tp // 2)], cwv, cw_sem
    )
    weights.start()
    for a, (src, dst) in enumerate(((lq, qb), (og, gb))):
        pltpu.make_async_copy(src.at[0, :, feat(head)], dst.at[pl.ds(0, ROWS)], q_r.at[a, 0]).start()
    for a, (src, dst) in enumerate(((lk, kb), (lv, vb))):
        pltpu.make_async_copy(
            src.at[0, :, feat(head)], dst.at[rows_at(core * ROWS, ROWS)], k_r.at[a, 0]
        ).start()

    with jax.named_scope("barrier"):
        pl.semaphore_wait(barrier, 24)

    def in_copy(a, src, dst, dst_start, slot, arrival):
        device, there = chip(slot, 1)
        return pltpu.make_async_remote_copy(
            src_ref=src.at[0, :, feat(there)],
            dst_ref=dst.at[rows_at(dst_start, ROWS)],
            send_sem=in_s.at[a],
            recv_sem=arrival,
            device_id=device,
            device_id_type=MESH,
        )

    def send_q(slot, carry):
        for a, (src, dst) in enumerate(((lq, qb), (og, gb))):
            in_copy(a, src, dst, slot * ROWS, slot, q_r.at[a, slot // GROUP]).start()
        return carry

    def send_k(slot, carry):
        row = slot * 2 * ROWS + core * ROWS
        for a, (src, dst) in enumerate(((lk, kb), (lv, vb))):
            in_copy(2 + a, src, dst, row, slot, k_r.at[a, slot // TILE_SLOTS]).start()
        return carry

    with jax.named_scope("send_inputs"):
        lax.fori_loop(1, HALF_SLOTS, send_q, 0)
        lax.fori_loop(1, 4, send_k, 0)

    def window(zz):
        return pl.ds(pl.multiple_of((7 * zz // 2) * HD, HD), WINDOW)

    for dz in range(1, 8):
        there = (z + dz) % 8
        pltpu.make_async_remote_copy(
            src_ref=hid.at[0, :, window(there)],
            dst_ref=hida.at[dz],
            send_sem=hid_s,
            recv_sem=hid_r,
            device_id={"dp": there},
            device_id_type=MESH,
        ).start()
    hida[0] = hid[0, :, window(z)]

    weights.wait()

    def cond_step(i, sums):
        r = pl.multiple_of(i * 512, 512)
        rows = hid[0, :, pl.ds(r, 512)]
        return (
            sums[0] + mm(rows, cwv[pl.ds(r, 512), 0, :], 1, 0),
            sums[1] + mm(rows, cwv[pl.ds(r, 512), 1, :], 1, 0),
        )

    nothing = jnp.zeros((COND, HD), F32)
    with jax.named_scope("condition_keys"):
        cond_k, cond_v = lax.fori_loop(0, 7, cond_step, (nothing, nothing))
    kb[pl.ds(KEYS, COND), :] = cond_k.astype(BF16)
    vb[pl.ds(KEYS, COND), :] = cond_v.astype(BF16)

    def take_queries(half):
        for group in (2 * half, 2 * half + 1):
            with jax.named_scope("wait_queries"):
                for a, dst in enumerate((qb, gb)):
                    arrived(dst.at[pl.ds(group * GROUP * ROWS, GROUP * ROWS)], q_r.at[a, group])
        qt[...] = qb[pl.ds(half * QB, QB), :].T
        gt[...] = gb[pl.ds(half * QB, QB), :].T
        dqa[...] = jnp.zeros_like(dqa)

    def pass_keys(tile):
        with jax.named_scope("wait_keys"):
            for a, dst in enumerate((kb, vb)):
                arrived(dst.at[pl.ds(0, TILE_SLOTS * ROWS)], k_r.at[a, tile])
        for i in range(TILE_SLOTS):
            for a, dst in enumerate((kb, vb)):
                mine = dst.at[rows_at((tile * TILE_SLOTS + i) * 2 * ROWS + core * ROWS, ROWS)]
                pltpu.make_async_remote_copy(
                    src_ref=mine,
                    dst_ref=mine,
                    send_sem=fw_s.at[a],
                    recv_sem=fw_r.at[a, tile],
                    device_id=partner,
                    device_id_type=MESH,
                ).start()

    def take_keys(tile):
        with jax.named_scope("wait_partner_keys"):
            for a, dst in enumerate((kb, vb)):
                arrived(dst.at[pl.ds(0, TILE_SLOTS * ROWS)], fw_r.at[a, tile])

    def forward(tile, stats, start, size):
        top, total, dots = stats
        keys = rows_at(start, size)
        scores = mm(kb[keys, :], qt[...], 1, 0)
        dprobs = mm(vb[keys, :], gt[...], 1, 0)
        top_new = jnp.maximum(top, jnp.ceil(jnp.max(scores, axis=0, keepdims=True) * SCALE2))
        e = jnp.exp2(scores * SCALE2 - top_new)
        shrink = jnp.exp2(top - top_new)
        total = total * shrink + jnp.sum(e, axis=0, keepdims=True)
        dots = dots * shrink + jnp.sum(e * dprobs, axis=0, keepdims=True)
        e_s[keys, :] = e.astype(BF16)
        dp_s[keys, :] = dprobs
        m_s[pl.ds(tile, 1), :] = top_new
        return top_new, total, dots

    def end_forward(stats):
        top, total, dots = stats
        inverse = 1.0 / total
        gi[...] = (gt[...].astype(F32) * inverse).astype(BF16)
        qi[...] = (qt[...].astype(F32) * (inverse * SCALE)).astype(BF16)
        return top, dots * inverse, inverse * SCALE

    def backward(tile, stats, start, size, first=False, pair=False):
        top, mean, _ = stats
        keys = rows_at(start, size)
        last = m_s[pl.ds(tile, 1), :]
        e = e_s[keys, :]
        if pair:
            step = jnp.exp2(m_s[pl.ds(tile - 1, 1), :] - last).astype(BF16)
            e = jnp.concatenate([e[: size // 2] * step, e[size // 2 :]], 0)
        factor = jnp.exp2(last - top)
        low = factor.astype(BF16)
        ds = (e.astype(F32) * (dp_s[keys, :] - mean)).astype(BF16)
        part_v = mm(e, gi[...] * low, 1, 1)
        va[keys, :] = part_v if first else va[keys, :] + part_v
        part_k = mm(ds, qi[...] * low, 1, 1)
        ka[keys, :] = part_k if first else ka[keys, :] + part_k
        dqa[...] += mm(kb[keys, :], ds, 0, 0) * factor

    def out_copy(a, src, dst, slot):
        device, _ = chip(slot, -1)
        return pltpu.make_async_remote_copy(
            src_ref=src,
            dst_ref=dst.at[0, :, feat(head)],
            send_sem=out_s.at[a],
            recv_sem=out_r.at[a],
            device_id=device,
            device_id_type=MESH,
        )

    def send_out(a, src, dst, slot):
        @pl.when(slot > 0)
        def _():
            out_copy(a, src, dst, slot).start()

        @pl.when(slot == 0)
        def _():
            pltpu.make_async_copy(src, dst.at[0, :, feat(head)], out_r.at[a]).start()

    def send_dq(half, stats):
        dqb[pl.ds(half * QB, QB), :] = (dqa[...] * stats[2]).T.astype(BF16)

        def one(slot, carry):
            send_out(0, dqb.at[rows_at(slot * ROWS, ROWS)], dq_o, slot)
            return carry

        lax.fori_loop(half * HALF_SLOTS, (half + 1) * HALF_SLOTS, one, 0)

    low = jnp.full((1, QB), -1e30, F32)
    zero = jnp.zeros((1, QB), F32)
    start = (low, zero, zero)

    def step_first(tile, stats):
        @pl.when(tile < TILES - 1)
        def _():
            pass_keys(tile + 1)

        @pl.when(tile == TILES - 2)
        def _():
            lax.fori_loop(HALF_SLOTS, SLOTS, send_q, 0)

        take_keys(tile)
        with jax.named_scope("forward_first"):
            return forward(tile, stats, tile * KT, KT)

    lax.fori_loop(4, 8, send_k, 0)
    take_queries(0)
    lax.fori_loop(8, 12, send_k, 0)
    stats = forward(TILES, start, KEYS, COND)
    pass_keys(0)
    lax.fori_loop(12, SLOTS, send_k, 0)
    stats = end_forward(lax.fori_loop(0, TILES, step_first, stats))

    def back_first(tile, carry):
        backward(2 * tile + 1, stats, tile * BT, BT, True, True)
        return carry

    backward(TILES, stats, KEYS, COND, True)
    with jax.named_scope("backward_first"):
        lax.fori_loop(0, BACK_TILES, back_first, 0)
    with jax.named_scope("send_dq"):
        send_dq(0, stats)

    def step_second(tile, stats):
        with jax.named_scope("forward_second"):
            return forward(tile, stats, tile * BT, BT)

    take_queries(1)
    stats = forward(TILES, start, KEYS, COND)
    stats = end_forward(lax.fori_loop(0, BACK_TILES, step_second, stats))

    backward(TILES, stats, KEYS, COND)

    @pl.when(core == 0)
    def _():
        c_st[...] = va[pl.ds(KEYS, COND), :].astype(BF16)

    @pl.when(core == 1)
    def _():
        c_st[...] = ka[pl.ds(KEYS, COND), :].astype(BF16)

    pltpu.make_async_remote_copy(
        src_ref=c_st, dst_ref=c_rx, send_sem=c1_s, recv_sem=c1_r, device_id=partner, device_id_type=MESH
    ).start()

    def cond_sum():
        arrived(c_rx, c1_r)

        @pl.when(core == 0)
        def _():
            cga[0] = (ka[pl.ds(KEYS, COND), :] + c_rx[...].astype(F32)).astype(BF16)

        @pl.when(core == 1)
        def _():
            cga[0] = (va[pl.ds(KEYS, COND), :] + c_rx[...].astype(F32)).astype(BF16)

        for dz in range(1, 8):
            pltpu.make_async_remote_copy(
                src_ref=cga.at[0],
                dst_ref=cga.at[dz],
                send_sem=cg_s,
                recv_sem=cg_r,
                device_id={"dp": (z + dz) % 8},
                device_id_type=MESH,
            ).start()

    def part_copy(dt):
        owner = (tp + dt) % 4
        return pltpu.make_async_remote_copy(
            src_ref=prod.at[pl.ds(pl.multiple_of((z % 2) * 64 + owner * 112, 16), 112)],
            dst_ref=w_o.at[tp],
            send_sem=w_s,
            recv_sem=w_r,
            device_id={"tp": owner},
            device_id_type=MESH,
        )

    def cond_product():
        arrived(hida.at[pl.ds(1, 7)], hid_r)
        arrived(cga.at[pl.ds(1, 7)], cg_r)
        prod[...] = mm(
            hida[...].reshape(8 * COND, WINDOW), cga[...].reshape(8 * COND, HD), 0, 0
        )
        for dt in range(1, 4):
            part_copy(dt).start()
        pltpu.make_async_copy(
            prod.at[pl.ds(pl.multiple_of((z % 2) * 64 + tp * 112, 16), 112)], w_o.at[tp], w_r
        ).start()

    def tile_slots(tile):
        return pl.ds(pl.multiple_of(tile * BACK_SLOTS, BACK_SLOTS), BACK_SLOTS)

    def swap(tile):
        for i in range(BACK_SLOTS):
            slot = tile * BACK_SLOTS + i
            theirs = rows_at(slot * 2 * ROWS + (1 - core) * ROWS, ROWS)
            st[0, slot] = ka[theirs, :].astype(BF16)
            st[1, slot] = va[theirs, :].astype(BF16)
        for a in range(2):
            pltpu.make_async_remote_copy(
                src_ref=st.at[a, tile_slots(tile)],
                dst_ref=rx.at[a, tile_slots(tile)],
                send_sem=ex_s.at[a],
                recv_sem=ex_r.at[a, tile],
                device_id=partner,
                device_id_type=MESH,
            ).start()

    def finish(tile):
        for a in range(2):
            arrived(rx.at[a, tile_slots(tile)], ex_r.at[a, tile])
        for i in range(BACK_SLOTS):
            slot = tile * BACK_SLOTS + i
            mine = rows_at(slot * 2 * ROWS + core * ROWS, ROWS)
            for a, (acc, dst) in enumerate(((ka, dk_o), (va, dv_o))):
                fin[a, slot] = (acc[mine, :] + rx[a, slot].astype(F32)).astype(BF16)
                send_out(1 + a, fin.at[a, slot], dst, slot)

    def back(tile, carry):
        with jax.named_scope("backward_tile"):
            backward(tile, stats, tile * BT, BT)
        swap(tile)

        @pl.when(tile > 0)
        def _():
            with jax.named_scope("finish"):
                finish(tile - 1)

        @pl.when(tile == 1)
        def _():
            with jax.named_scope("condition_sum"):
                cond_sum()

        return carry

    lax.fori_loop(0, BACK_TILES, back, 0)
    with jax.named_scope("send_dq"):
        send_dq(1, stats)
    with jax.named_scope("finish"):
        finish(BACK_TILES - 1)
    with jax.named_scope("condition_product"):
        cond_product()

    with jax.named_scope("drain"):
        sent = pl.ds(0, (SLOTS - 1) * ROWS)
        for a in range(4):
            arrived(qb.at[sent], in_s.at[a])
        for a in range(2):
            arrived(qb, fw_s.at[a])
            arrived(st.at[a], ex_s.at[a])
        arrived(c_st, c1_s)
        arrived(hida.at[pl.ds(1, 7)], hid_s)
        arrived(cga.at[pl.ds(1, 7)], cg_s)
        for a in range(3):
            arrived(dqb.at[sent], out_s.at[a])
        arrived(w_o.at[pl.ds(0, 3)], w_s)
        arrived(w_o, w_r)
        for a, dst in enumerate((dq_o, dk_o, dv_o)):
            arrived(dst.at[0], out_r.at[a])


def place(dq, dk, dv, parts, dq_o, dk_o, dv_o, w_o, held, held_w, in_s, out_s, w_s):
    fetch_w = pltpu.make_async_copy(parts, held_w, w_s)
    fetches = [
        pltpu.make_async_copy(src, held.at[a], in_s.at[a]) for a, src in enumerate((dq, dk, dv))
    ]
    stores = [
        pltpu.make_async_copy(held.at[a], dst, out_s.at[a])
        for a, dst in enumerate((dq_o, dk_o, dv_o))
    ]
    for fetch in fetches:
        fetch.start()
    fetch_w.start()
    for fetch, store in zip(fetches, stores):
        fetch.wait()
        store.start()
    fetch_w.wait()
    for half in range(2):
        for array in range(2):
            w_o[:, array, half * HD : (half + 1) * HD] = held_w[2 * half + array]
    for store in stores:
        store.wait()


def on_device(latent_query, latent_key, latent_value, out_grad, query_hidden, cond_weight):
    anywhere = pl.BlockSpec(memory_space=pl.ANY)
    token = jax.ShapeDtypeStruct(latent_query.shape, BF16)
    dma = pltpu.SemaphoreType.DMA
    total_keys = KEYS + COND
    grads = pl.pallas_call(
        kernel,
        name="attention_backward",
        out_shape=(token, token, token, jax.ShapeDtypeStruct((4, 112, HD), F32)),
        in_specs=[anywhere] * 4 + [pl.BlockSpec(memory_space=pltpu.VMEM), anywhere],
        out_specs=(anywhere,) * 4,
        scratch_shapes=[
            pltpu.VMEM((2 * QB, HD), BF16),
            pltpu.VMEM((2 * QB, HD), BF16),
            pltpu.VMEM((total_keys, HD), BF16),
            pltpu.VMEM((total_keys, HD), BF16),
            pltpu.VMEM((HD, QB), BF16),
            pltpu.VMEM((HD, QB), BF16),
            pltpu.VMEM((HD, QB), BF16),
            pltpu.VMEM((HD, QB), BF16),
            pltpu.VMEM((total_keys, QB), BF16),
            pltpu.VMEM((total_keys, QB), F32),
            pltpu.VMEM((16, QB), F32),
            pltpu.VMEM((total_keys, HD), F32),
            pltpu.VMEM((total_keys, HD), F32),
            pltpu.VMEM((HD, QB), F32),
            pltpu.VMEM((2 * QB, HD), BF16),
            pltpu.VMEM((2, SLOTS, ROWS, HD), BF16),
            pltpu.VMEM((2, SLOTS, ROWS, HD), BF16),
            pltpu.VMEM((2, SLOTS, ROWS, HD), BF16),
            pltpu.VMEM((cond_weight.shape[0], 2, HD), BF16),
            pltpu.VMEM((8, COND, WINDOW), BF16),
            pltpu.VMEM((COND, HD), BF16),
            pltpu.VMEM((COND, HD), BF16),
            pltpu.VMEM((8, COND, HD), BF16),
            pltpu.VMEM((WINDOW, HD), F32),
            dma((4,)), dma((2, SLOTS // GROUP)), dma((2, TILES)),
            dma((2,)), dma((2, TILES)),
            dma((2,)), dma((2, BACK_TILES)),
            dma((3,)), dma((3,)),
            dma, dma,
            dma, dma,
            dma, dma,
            dma, dma,
            dma,
        ],
        compiler_params=pltpu.CompilerParams(
            collective_id=0, has_side_effects=True, vmem_limit_bytes=60 << 20
        ),
    )(latent_query, latent_key, latent_value, out_grad, query_hidden, cond_weight)
    weight = jax.ShapeDtypeStruct((112, 2, 2 * HD), F32)
    return pl.pallas_call(
        place,
        name="place_outputs",
        out_shape=(token, token, token, weight),
        in_specs=[anywhere] * 4,
        out_specs=(anywhere,) * 3 + (pl.BlockSpec(memory_space=pltpu.VMEM),),
        scratch_shapes=[
            pltpu.VMEM((3,) + latent_query.shape, BF16),
            pltpu.VMEM((4, 112, HD), F32),
            dma((3,)), dma((3,)), dma,
        ],
    )(*grads)


def solution(mesh):
    placed = (
        P("dp", ("seq", "tp"), None),
        P("dp", ("seq", "tp"), None),
        P("dp", ("seq", "tp"), None),
        P("dp", ("seq", "tp"), None),
        P("dp", None, None),
        P(None, None, "seq"),
    )
    return jax.shard_map(
        on_device,
        mesh=mesh,
        in_specs=placed,
        out_specs=(
            P("dp", ("seq", "tp"), None),
            P("dp", ("seq", "tp"), None),
            P("dp", ("seq", "tp"), None),
            P(("dp", "tp"), None, "seq"),
        ),
        check_vma=False,
    )
```

```python
import jax
import jax.numpy as jnp
from jax import lax
from jax.experimental import pallas as pl
from jax.experimental.pallas import tpu as pltpu
from jax.sharding import PartitionSpec as P

HD = 128
MESH = pl.DeviceIdType.MESH
F32 = jnp.float32
BF16 = jnp.bfloat16
SCALE = HD ** (-0.5)
SCALE2 = SCALE * 1.4426950408889634
ROWS = 128
SLOTS = 16
QB = 1024
KT = 512
BT = 2 * KT
KEYS = 4096
COND = 64
TILES = KEYS // KT
TILE_SLOTS = SLOTS // TILES
BACK_TILES = KEYS // BT
BACK_SLOTS = SLOTS // BACK_TILES
HALF_SLOTS = QB // ROWS
GROUP = 4
WINDOW = 512


def mm(a, b, ca, cb):
    return lax.dot_general(a, b, (((ca,), (cb,)), ((), ())), preferred_element_type=F32)


OFFSETS = (
    (0, 0), (0, 1), (1, 0), (0, 3), (3, 0), (1, 1), (3, 3), (2, 0),
    (0, 2), (1, 3), (3, 1), (1, 2), (2, 1), (3, 2), (2, 3), (2, 2),
)


def pick(slot, values):
    if isinstance(slot, int):
        return values[slot]
    out = values[0]
    for k in range(1, len(values)):
        if values[k] != values[k - 1]:
            out = jnp.where(slot >= k, values[k], out)
    return out


def offset_of(slot):
    return pick(slot, [dx for dx, _ in OFFSETS]), pick(slot, [dy for _, dy in OFFSETS])


def rows_at(start, size):
    if isinstance(start, int):
        return pl.ds(start, size)
    return pl.ds(pl.multiple_of(start, 64), size)


def arrived(ref, sem):
    pltpu.make_async_copy(ref, ref, sem).wait()


def kernel(
    lq, lk, lv, og, hidden, cw,
    dq_o, dk_o, dv_o, w_o,
    qb, gb, kb, vb, qt, gt, qi, gi, e_s, dp_s, m_s, ka, va, dqa, dqb,
    st, rx, fin, cwv, hid, hida, c_st, c_rx, cga, prod,
    in_s, q_r, k_r, fw_s, fw_r, ex_s, ex_r, out_s, out_r,
    hid_s, hid_r, c1_s, c1_r, cg_s, cg_r, w_s, w_r, cw_sem, hid_sem,
):
    z = lax.axis_index("dp")
    seq = lax.axis_index("seq")
    tp = lax.axis_index("tp")
    x = (seq // 4) * 2 + tp // 2
    y = seq % 4
    core = tp % 2
    head = 2 * seq + tp // 2
    partner = {"tp": (tp // 2) * 2 + 1 - core}

    def chip(slot, sign):
        dx, dy = offset_of(slot)
        cx = (x + sign * dx + 4) % 4
        cy = (y + sign * dy + 4) % 4
        cseq = (cx // 2) * 4 + cy
        return {"seq": cseq, "tp": (cx % 2) * 2 + core}, 2 * cseq + cx % 2

    def feat(index):
        return pl.ds(pl.multiple_of(index * HD, HD), HD)

    barrier = pltpu.get_barrier_semaphore()

    for slot in range(1, SLOTS):
        device, _ = chip(slot, 1)
        pl.semaphore_signal(barrier, inc=1, device_id=device, device_id_type=MESH)
    pl.semaphore_signal(barrier, inc=1, device_id=partner, device_id_type=MESH)
    pl.semaphore_signal(barrier, inc=1, device_id={"tp": 3 - tp}, device_id_type=MESH)
    for dz in range(1, 8):
        pl.semaphore_signal(
            barrier, inc=1, device_id={"dp": (z + dz) % 8}, device_id_type=MESH
        )

    weights = pltpu.make_async_copy(
        cw.at[:, :, feat(tp // 2)], cwv, cw_sem
    )
    weights.start()
    rows = pltpu.make_async_copy(hidden, hid, hid_sem)
    rows.start()
    for a, (src, dst) in enumerate(((lq, qb), (og, gb))):
        pltpu.make_async_copy(src.at[0, :, feat(head)], dst.at[pl.ds(0, ROWS)], q_r.at[a, 0]).start()
    for a, (src, dst) in enumerate(((lk, kb), (lv, vb))):
        pltpu.make_async_copy(
            src.at[0, :, feat(head)], dst.at[rows_at(core * ROWS, ROWS)], k_r.at[a, 0]
        ).start()

    with jax.named_scope("barrier"):
        pl.semaphore_wait(barrier, 24)

    def in_copy(a, src, dst, dst_start, slot, arrival):
        device, there = chip(slot, 1)
        return pltpu.make_async_remote_copy(
            src_ref=src.at[0, :, feat(there)],
            dst_ref=dst.at[rows_at(dst_start, ROWS)],
            send_sem=in_s.at[a],
            recv_sem=arrival,
            device_id=device,
            device_id_type=MESH,
        )

    def send_q(slots):
        for slot in slots:
            for a, (src, dst) in enumerate(((lq, qb), (og, gb))):
                in_copy(a, src, dst, slot * ROWS, slot, q_r.at[a, slot // GROUP]).start()

    def send_k(slots):
        for slot in slots:
            row = slot * 2 * ROWS + core * ROWS
            for a, (src, dst) in enumerate(((lk, kb), (lv, vb))):
                in_copy(2 + a, src, dst, row, slot, k_r.at[a, slot // TILE_SLOTS]).start()

    with jax.named_scope("send_inputs"):
        send_q(range(1, HALF_SLOTS))
        send_k(range(1, SLOTS))

    def window(zz):
        return pl.ds(pl.multiple_of((7 * zz // 2) * HD, HD), WINDOW)

    rows.wait()
    for dz in range(1, 8):
        there = (z + dz) % 8
        pltpu.make_async_remote_copy(
            src_ref=hid.at[0, :, window(there)],
            dst_ref=hida.at[dz],
            send_sem=hid_s,
            recv_sem=hid_r,
            device_id={"dp": there},
            device_id_type=MESH,
        ).start()
    hida[0] = hid[0, :, window(z)]
    weights.wait()

    def cond_step(i, sums):
        r = pl.multiple_of(i * 512, 512)
        rows = hid[0, :, pl.ds(r, 512)]
        return (
            sums[0] + mm(rows, cwv[pl.ds(r, 512), 0, :], 1, 0),
            sums[1] + mm(rows, cwv[pl.ds(r, 512), 1, :], 1, 0),
        )

    nothing = jnp.zeros((COND, HD), F32)
    with jax.named_scope("condition_keys"):
        cond_k, cond_v = lax.fori_loop(0, 7, cond_step, (nothing, nothing))
    kb[pl.ds(KEYS, COND), :] = cond_k.astype(BF16)
    vb[pl.ds(KEYS, COND), :] = cond_v.astype(BF16)

    def take_queries(half):
        for group in (2 * half, 2 * half + 1):
            with jax.named_scope("wait_queries"):
                for a, dst in enumerate((qb, gb)):
                    arrived(dst.at[pl.ds(group * GROUP * ROWS, GROUP * ROWS)], q_r.at[a, group])
        qt[half] = qb[pl.ds(half * QB, QB), :].T
        gt[half] = gb[pl.ds(half * QB, QB), :].T
        dqa[half] = jnp.zeros((HD, QB), F32)

    def pass_keys(tile):
        with jax.named_scope("wait_keys"):
            for a, dst in enumerate((kb, vb)):
                arrived(dst.at[pl.ds(0, TILE_SLOTS * ROWS)], k_r.at[a, tile])
        for i in range(TILE_SLOTS):
            for a, dst in enumerate((kb, vb)):
                mine = dst.at[rows_at((tile * TILE_SLOTS + i) * 2 * ROWS + core * ROWS, ROWS)]
                pltpu.make_async_remote_copy(
                    src_ref=mine,
                    dst_ref=mine,
                    send_sem=fw_s.at[a],
                    recv_sem=fw_r.at[a, tile],
                    device_id=partner,
                    device_id_type=MESH,
                ).start()

    def take_keys(tile):
        with jax.named_scope("wait_partner_keys"):
            for a, dst in enumerate((kb, vb)):
                arrived(dst.at[pl.ds(0, TILE_SLOTS * ROWS)], fw_r.at[a, tile])

    def forward(half, tile, stats, start, size):
        top, total, dots = stats
        keys = rows_at(start, size)
        scores = mm(kb[keys, :], qt[half], 1, 0)
        dprobs = mm(vb[keys, :], gt[half], 1, 0)
        top_new = jnp.maximum(top, jnp.ceil(jnp.max(scores, axis=0, keepdims=True) * SCALE2))
        e = jnp.exp2(scores * SCALE2 - top_new)
        shrink = jnp.exp2(top - top_new)
        total = total * shrink + jnp.sum(e, axis=0, keepdims=True)
        dots = dots * shrink + jnp.sum(e * dprobs, axis=0, keepdims=True)
        e_s[half, keys, :] = e.astype(BF16)
        if half == 0:
            dp_s[keys, :] = dprobs
        m_s[half, pl.ds(tile, 1), :] = top_new
        return top_new, total, dots

    def end_forward(half, stats):
        top, total, dots = stats
        inverse = 1.0 / total
        gi[half] = (gt[half].astype(F32) * inverse).astype(BF16)
        qi[half] = (qt[half].astype(F32) * (inverse * SCALE)).astype(BF16)
        return top, dots * inverse, inverse * SCALE

    def backward(half, tile, stats, start, size, first=False, pair=False):
        top, mean, _ = stats
        keys = rows_at(start, size)
        last = m_s[half, pl.ds(tile, 1), :]
        e = e_s[half, keys, :]
        if pair:
            step = jnp.exp2(m_s[half, pl.ds(tile - 1, 1), :] - last).astype(BF16)
            e = jnp.concatenate([e[: size // 2] * step, e[size // 2 :]], 0)
        factor = jnp.exp2(last - top)
        low = factor.astype(BF16)
        part_v = mm(e, gi[half] * low, 1, 1)
        va[keys, :] = part_v if first else va[keys, :] + part_v
        dprobs = dp_s[keys, :] if half == 0 else mm(vb[keys, :], gt[half], 1, 0)
        ds = (e.astype(F32) * (dprobs - mean)).astype(BF16)
        part_k = mm(ds, qi[half] * low, 1, 1)
        ka[keys, :] = part_k if first else ka[keys, :] + part_k
        dqa[half] += mm(kb[keys, :], ds, 0, 0) * factor

    def out_copy(a, src, dst, slot):
        device, _ = chip(slot, -1)
        return pltpu.make_async_remote_copy(
            src_ref=src,
            dst_ref=dst.at[0, :, feat(head)],
            send_sem=out_s.at[a],
            recv_sem=out_r.at[a],
            device_id=device,
            device_id_type=MESH,
        )

    def send_out(a, src, dst, slot):
        def here():
            pltpu.make_async_copy(src, dst.at[0, :, feat(head)], out_r.at[a]).start()

        def there():
            out_copy(a, src, dst, slot).start()

        if isinstance(slot, int):
            there() if slot else here()
        else:
            pl.when(slot > 0)(there)
            pl.when(slot == 0)(here)

    def send_dq(half, stats):
        with jax.named_scope("send_dq"):
            dqb[pl.ds(half * QB, QB), :] = (dqa[half] * stats[2]).T.astype(BF16)
            for slot in range(half * HALF_SLOTS, (half + 1) * HALF_SLOTS):
                send_out(0, dqb.at[pl.ds(slot * ROWS, ROWS)], dq_o, slot)

    low = jnp.full((1, QB), -1e30, F32)
    zero = jnp.zeros((1, QB), F32)
    start = (low, zero, zero)

    def step_first(tile, stats):
        @pl.when(tile < TILES - 1)
        def _():
            pass_keys(tile + 1)

        @pl.when(tile == 3)
        def _():
            send_q(range(HALF_SLOTS, SLOTS))

        take_keys(tile)
        with jax.named_scope("forward_first"):
            return forward(0, tile, stats, tile * KT, KT)

    take_queries(0)
    first = forward(0, TILES, start, KEYS, COND)
    pass_keys(0)
    first = end_forward(0, lax.fori_loop(0, TILES, step_first, first))

    last = BACK_TILES - 1
    with jax.named_scope("backward_first"):
        backward(0, TILES, first, KEYS, COND, True)
        for tile in (last, last - 1):
            backward(0, 2 * tile + 1, first, tile * BT, BT, True, True)

    def step_second(tile, stats):
        with jax.named_scope("forward_second"):
            return forward(1, tile, stats, tile * BT, BT)

    take_queries(1)
    second = forward(1, BACK_TILES, start, KEYS, COND)
    second = end_forward(1, lax.fori_loop(0, BACK_TILES, step_second, second))
    backward(1, BACK_TILES, second, KEYS, COND)

    @pl.when(core == 0)
    def _():
        c_st[...] = va[pl.ds(KEYS, COND), :].astype(BF16)

    @pl.when(core == 1)
    def _():
        c_st[...] = ka[pl.ds(KEYS, COND), :].astype(BF16)

    pltpu.make_async_remote_copy(
        src_ref=c_st, dst_ref=c_rx, send_sem=c1_s, recv_sem=c1_r, device_id=partner, device_id_type=MESH
    ).start()

    def cond_sum():
        arrived(c_rx, c1_r)

        @pl.when(core == 0)
        def _():
            cga[0] = (ka[pl.ds(KEYS, COND), :] + c_rx[...].astype(F32)).astype(BF16)

        @pl.when(core == 1)
        def _():
            cga[0] = (va[pl.ds(KEYS, COND), :] + c_rx[...].astype(F32)).astype(BF16)

        for dz in range(1, 8):
            pltpu.make_async_remote_copy(
                src_ref=cga.at[0],
                dst_ref=cga.at[dz],
                send_sem=cg_s,
                recv_sem=cg_r,
                device_id={"dp": (z + dz) % 8},
                device_id_type=MESH,
            ).start()

    def part_copy(dt):
        owner = (tp + dt) % 4
        return pltpu.make_async_remote_copy(
            src_ref=prod.at[pl.ds(pl.multiple_of((z % 2) * 64 + owner * 112, 16), 112)],
            dst_ref=w_o.at[tp],
            send_sem=w_s,
            recv_sem=w_r,
            device_id={"tp": owner},
            device_id_type=MESH,
        )

    def cond_product():
        arrived(hida.at[pl.ds(1, 7)], hid_r)
        arrived(cga.at[pl.ds(1, 7)], cg_r)
        prod[...] = mm(
            hida[...].reshape(8 * COND, WINDOW), cga[...].reshape(8 * COND, HD), 0, 0
        ).astype(BF16)
        for dt in range(1, 4):
            part_copy(dt).start()
        pltpu.make_async_copy(
            prod.at[pl.ds(pl.multiple_of((z % 2) * 64 + tp * 112, 16), 112)], w_o.at[tp], w_r
        ).start()

    def swap(unit, slot, count):
        for i in range(count):
            theirs = rows_at((slot + i) * 2 * ROWS + (1 - core) * ROWS, ROWS)
            st[0, slot + i] = ka[theirs, :].astype(BF16)
            st[1, slot + i] = va[theirs, :].astype(BF16)
        for a in range(2):
            part = pl.ds(slot, count)
            pltpu.make_async_remote_copy(
                src_ref=st.at[a, part],
                dst_ref=rx.at[a, part],
                send_sem=ex_s.at[a],
                recv_sem=ex_r.at[a, unit],
                device_id=partner,
                device_id_type=MESH,
            ).start()

    def finish(unit, slot, count):
        with jax.named_scope("finish"):
            for a in range(2):
                arrived(rx.at[a, pl.ds(slot, count)], ex_r.at[a, unit])
            for i in range(count):
                mine = rows_at((slot + i) * 2 * ROWS + core * ROWS, ROWS)
                for a, (acc, dst) in enumerate(((ka, dk_o), (va, dv_o))):
                    fin[a, slot + i] = (acc[mine, :] + rx[a, slot + i].astype(F32)).astype(BF16)
                    send_out(1 + a, fin.at[a, slot + i], dst, slot + i)

    for unit in range(2):
        with jax.named_scope("backward_tile"):
            backward(1, last, second, last * BT + unit * KT, KT)
        swap(unit, last * BACK_SLOTS + unit * 2, 2)
    with jax.named_scope("condition_sum"):
        cond_sum()
    finish(0, last * BACK_SLOTS, 2)

    with jax.named_scope("backward_tile"):
        backward(1, last - 1, second, (last - 1) * BT, BT)
    swap(2, (last - 1) * BACK_SLOTS, BACK_SLOTS)
    finish(1, last * BACK_SLOTS + 2, 2)

    def back(step, carry):
        tile = last - step
        with jax.named_scope("backward_tile"):
            backward(1, tile, second, tile * BT, BT, True)

        @pl.when(tile == 0)
        def _():
            send_dq(1, second)

        @pl.when(step == 2)
        def _():
            with jax.named_scope("condition_product"):
                cond_product()

        finish(step, (tile + 1) * BACK_SLOTS, BACK_SLOTS)
        with jax.named_scope("backward_tile"):
            backward(0, 2 * tile + 1, first, tile * BT, BT, False, True)
        swap(step + 1, tile * BACK_SLOTS, BACK_SLOTS)
        return carry

    lax.fori_loop(2, BACK_TILES, back, 0)
    send_dq(0, first)
    finish(BACK_TILES, 0, BACK_SLOTS)

    with jax.named_scope("drain"):
        sent = pl.ds(0, (SLOTS - 1) * ROWS)
        for a in range(4):
            arrived(qb.at[sent], in_s.at[a])
        for a in range(2):
            arrived(qb, fw_s.at[a])
            arrived(st.at[a], ex_s.at[a])
        arrived(c_st, c1_s)
        arrived(hida.at[pl.ds(1, 7)], hid_s)
        arrived(cga.at[pl.ds(1, 7)], cg_s)
        for a in range(3):
            arrived(dqb.at[sent], out_s.at[a])
    with jax.named_scope("drain_weight"):
        arrived(w_o.at[pl.ds(0, 3)], w_s)
        arrived(w_o, w_r)
    with jax.named_scope("drain_key"):
        arrived(dk_o.at[0], out_r.at[1])
    with jax.named_scope("drain_value"):
        arrived(dv_o.at[0], out_r.at[2])
    with jax.named_scope("drain_query"):
        arrived(dq_o.at[0], out_r.at[0])


def place(dq, dk, dv, parts, dq_o, dk_o, dv_o, w_o, held, held_w, full_w, in_s, out_s, w_s):
    fetch_w = pltpu.make_async_copy(parts, held_w, w_s.at[0])
    store_w = pltpu.make_async_copy(full_w, w_o, w_s.at[1])
    fetches = [
        pltpu.make_async_copy(src, held.at[a], in_s.at[a]) for a, src in enumerate((dq, dk, dv))
    ]
    stores = [
        pltpu.make_async_copy(held.at[a], dst, out_s.at[a])
        for a, dst in enumerate((dq_o, dk_o, dv_o))
    ]
    fetch_w.start()
    for fetch in fetches:
        fetch.start()
    fetch_w.wait()
    for half in range(2):
        for array in range(2):
            columns = slice(half * HD, (half + 1) * HD)
            full_w[:, array, columns] = held_w[2 * half + array].astype(F32)
    store_w.start()
    for fetch, store in zip(fetches, stores):
        fetch.wait()
        store.start()
    store_w.wait()
    for store in stores:
        store.wait()


def on_device(latent_query, latent_key, latent_value, out_grad, query_hidden, cond_weight):
    anywhere = pl.BlockSpec(memory_space=pl.ANY)
    token = jax.ShapeDtypeStruct(latent_query.shape, BF16)
    dma = pltpu.SemaphoreType.DMA
    total_keys = KEYS + COND
    grads = pl.pallas_call(
        kernel,
        name="attention_backward",
        out_shape=(token, token, token, jax.ShapeDtypeStruct((4, 112, HD), BF16)),
        in_specs=[anywhere] * 6,
        out_specs=(anywhere,) * 4,
        scratch_shapes=[
            pltpu.VMEM((2 * QB, HD), BF16),
            pltpu.VMEM((2 * QB, HD), BF16),
            pltpu.VMEM((total_keys, HD), BF16),
            pltpu.VMEM((total_keys, HD), BF16),
            pltpu.VMEM((2, HD, QB), BF16),
            pltpu.VMEM((2, HD, QB), BF16),
            pltpu.VMEM((2, HD, QB), BF16),
            pltpu.VMEM((2, HD, QB), BF16),
            pltpu.VMEM((2, total_keys, QB), BF16),
            pltpu.VMEM((total_keys, QB), F32),
            pltpu.VMEM((2, 16, QB), F32),
            pltpu.VMEM((total_keys, HD), F32),
            pltpu.VMEM((total_keys, HD), F32),
            pltpu.VMEM((2, HD, QB), F32),
            pltpu.VMEM((2 * QB, HD), BF16),
            pltpu.VMEM((2, SLOTS, ROWS, HD), BF16),
            pltpu.VMEM((2, SLOTS, ROWS, HD), BF16),
            pltpu.VMEM((2, SLOTS, ROWS, HD), BF16),
            pltpu.VMEM((cond_weight.shape[0], 2, HD), BF16),
            pltpu.VMEM(query_hidden.shape, BF16),
            pltpu.VMEM((8, COND, WINDOW), BF16),
            pltpu.VMEM((COND, HD), BF16),
            pltpu.VMEM((COND, HD), BF16),
            pltpu.VMEM((8, COND, HD), BF16),
            pltpu.VMEM((WINDOW, HD), BF16),
            dma((4,)), dma((2, SLOTS // GROUP)), dma((2, TILES)),
            dma((2,)), dma((2, TILES)),
            dma((2,)), dma((2, BACK_TILES + 1)),
            dma((3,)), dma((3,)),
            dma, dma,
            dma, dma,
            dma, dma,
            dma, dma,
            dma, dma,
        ],
        compiler_params=pltpu.CompilerParams(
            collective_id=0, has_side_effects=True, vmem_limit_bytes=60 << 20
        ),
    )(latent_query, latent_key, latent_value, out_grad, query_hidden, cond_weight)
    weight = jax.ShapeDtypeStruct((112, 2, 2 * HD), F32)
    return pl.pallas_call(
        place,
        name="place_outputs",
        out_shape=(token, token, token, weight),
        in_specs=[anywhere] * 4,
        out_specs=(anywhere,) * 4,
        scratch_shapes=[
            pltpu.VMEM((3,) + latent_query.shape, BF16),
            pltpu.VMEM((4, 112, HD), BF16),
            pltpu.VMEM((112, 2, 2 * HD), F32),
            dma((3,)), dma((3,)), dma((2,)),
        ],
    )(*grads)


def solution(mesh):
    placed = (
        P("dp", ("seq", "tp"), None),
        P("dp", ("seq", "tp"), None),
        P("dp", ("seq", "tp"), None),
        P("dp", ("seq", "tp"), None),
        P("dp", None, None),
        P(None, None, "seq"),
    )
    return jax.shard_map(
        on_device,
        mesh=mesh,
        in_specs=placed,
        out_specs=(
            P("dp", ("seq", "tp"), None),
            P("dp", ("seq", "tp"), None),
            P("dp", ("seq", "tp"), None),
            P(("dp", "tp"), None, "seq"),
        ),
        check_vma=False,
    )
```

```python
import jax
import jax.numpy as jnp
from jax import lax
from jax.experimental import pallas as pl
from jax.experimental.pallas import tpu as pltpu
from jax.sharding import PartitionSpec as P

HD = 128
MESH = pl.DeviceIdType.MESH
F32 = jnp.float32
BF16 = jnp.bfloat16
SCALE = HD ** (-0.5)
LOG2E = 1.4426950408889634
ROWS = 128
SLOTS = 16
QB = 1024
KT = 512
BT = 2 * KT
KEYS = 4096
COND = 64
TILES = KEYS // KT
TILE_SLOTS = SLOTS // TILES
BACK_TILES = KEYS // BT
BACK_SLOTS = SLOTS // BACK_TILES
KEPT = BACK_TILES - 2
HALF_SLOTS = QB // ROWS
GROUP = 4
WINDOW = 512


def mm(a, b, ca, cb):
    return lax.dot_general(a, b, (((ca,), (cb,)), ((), ())), preferred_element_type=F32)


OFFSETS = (
    (0, 0), (0, 1), (1, 0), (0, 3), (3, 0), (1, 1), (3, 3), (2, 0),
    (0, 2), (1, 3), (3, 1), (1, 2), (2, 1), (3, 2), (2, 3), (2, 2),
)


def pick(slot, values):
    if isinstance(slot, int):
        return values[slot]
    out = values[0]
    for k in range(1, len(values)):
        if values[k] != values[k - 1]:
            out = jnp.where(slot >= k, values[k], out)
    return out


def offset_of(slot):
    return pick(slot, [dx for dx, _ in OFFSETS]), pick(slot, [dy for _, dy in OFFSETS])


def rows_at(start, size):
    if isinstance(start, int):
        return pl.ds(start, size)
    return pl.ds(pl.multiple_of(start, 64), size)


def arrived(ref, sem):
    pltpu.make_async_copy(ref, ref, sem).wait()


def kernel(
    lq, lk, lv, og, hidden, cw,
    dq_o, dk_o, dv_o, w_o,
    qb, gb, kb, vb, qt, gt, qi, gi, e_s, dp_s, dp_t, m_s, ka, va, dqa,
    st, rx, cwv, hid, hida, c_st, c_rx, cga, prod,
    in_s, q_r, k_r, fw_s, fw_r, ex_s, ex_r, out_s, out_r,
    hid_s, hid_r, c1_s, c1_r, cg_s, cg_r, w_s, w_r, cw_sem, hid_sem,
):
    z = lax.axis_index("dp")
    seq = lax.axis_index("seq")
    tp = lax.axis_index("tp")
    x = (seq // 4) * 2 + tp // 2
    y = seq % 4
    core = tp % 2
    head = 2 * seq + tp // 2
    partner = {"tp": (tp // 2) * 2 + 1 - core}

    def chip(slot, sign):
        dx, dy = offset_of(slot)
        cx = (x + sign * dx + 4) % 4
        cy = (y + sign * dy + 4) % 4
        cseq = (cx // 2) * 4 + cy
        return {"seq": cseq, "tp": (cx % 2) * 2 + core}, 2 * cseq + cx % 2

    def feat(index):
        return pl.ds(pl.multiple_of(index * HD, HD), HD)

    barrier = pltpu.get_barrier_semaphore()

    for slot in range(1, SLOTS):
        device, _ = chip(slot, 1)
        pl.semaphore_signal(barrier, inc=1, device_id=device, device_id_type=MESH)
    pl.semaphore_signal(barrier, inc=1, device_id=partner, device_id_type=MESH)
    pl.semaphore_signal(barrier, inc=1, device_id={"tp": 3 - tp}, device_id_type=MESH)
    for dz in range(1, 8):
        pl.semaphore_signal(
            barrier, inc=1, device_id={"dp": (z + dz) % 8}, device_id_type=MESH
        )

    weights = pltpu.make_async_copy(
        cw.at[:, :, feat(tp // 2)], cwv, cw_sem
    )
    weights.start()
    rows = pltpu.make_async_copy(hidden, hid, hid_sem)
    rows.start()
    for a, (src, dst) in enumerate(((lq, qb), (og, gb))):
        pltpu.make_async_copy(src.at[0, :, feat(head)], dst.at[pl.ds(0, ROWS)], q_r.at[a, 0]).start()
    for a, (src, dst) in enumerate(((lk, kb), (lv, vb))):
        pltpu.make_async_copy(
            src.at[0, :, feat(head)], dst.at[rows_at(core * ROWS, ROWS)], k_r.at[a, 0]
        ).start()

    with jax.named_scope("barrier"):
        pl.semaphore_wait(barrier, 24)

    def in_copy(a, src, dst, dst_start, slot, arrival):
        device, there = chip(slot, 1)
        return pltpu.make_async_remote_copy(
            src_ref=src.at[0, :, feat(there)],
            dst_ref=dst.at[rows_at(dst_start, ROWS)],
            send_sem=in_s.at[a],
            recv_sem=arrival,
            device_id=device,
            device_id_type=MESH,
        )

    def send_q(slots):
        for slot in slots:
            for a, (src, dst) in enumerate(((lq, qb), (og, gb))):
                in_copy(a, src, dst, slot * ROWS, slot, q_r.at[a, slot // GROUP]).start()

    def send_k(slots):
        for slot in slots:
            row = slot * 2 * ROWS + core * ROWS
            for a, (src, dst) in enumerate(((lk, kb), (lv, vb))):
                in_copy(2 + a, src, dst, row, slot, k_r.at[a, slot // TILE_SLOTS]).start()

    with jax.named_scope("send_inputs"):
        for slot in range(1, SLOTS):
            if slot < HALF_SLOTS:
                send_q([slot])
            send_k([slot])

    def window(zz):
        return pl.ds(pl.multiple_of((7 * zz // 2) * HD, HD), WINDOW)

    rows.wait()
    for dz in range(1, 8):
        there = (z + dz) % 8
        pltpu.make_async_remote_copy(
            src_ref=hid.at[0, :, window(there)],
            dst_ref=hida.at[dz],
            send_sem=hid_s,
            recv_sem=hid_r,
            device_id={"dp": there},
            device_id_type=MESH,
        ).start()
    hida[0] = hid[0, :, window(z)]
    weights.wait()

    def cond_step(i, sums):
        r = pl.multiple_of(i * 512, 512)
        rows = hid[0, :, pl.ds(r, 512)]
        return (
            sums[0] + mm(rows, cwv[pl.ds(r, 512), 0, :], 1, 0),
            sums[1] + mm(rows, cwv[pl.ds(r, 512), 1, :], 1, 0),
        )

    nothing = jnp.zeros((COND, HD), F32)
    with jax.named_scope("condition_keys"):
        cond_k, cond_v = lax.fori_loop(0, 7, cond_step, (nothing, nothing))
    kb[pl.ds(KEYS, COND), :] = cond_k.astype(BF16)
    vb[pl.ds(KEYS, COND), :] = cond_v.astype(BF16)

    def take_queries(half):
        for group in (2 * half, 2 * half + 1):
            with jax.named_scope("wait_queries"):
                for a, dst in enumerate((qb, gb)):
                    arrived(dst.at[pl.ds(group * GROUP * ROWS, GROUP * ROWS)], q_r.at[a, group])
        scaled = qb[pl.ds(half * QB, QB), :].T.astype(F32) * (SCALE * LOG2E)
        high = scaled.astype(BF16)
        qt[half, :HD] = high
        qt[half, HD:] = (scaled - high.astype(F32)).astype(BF16)
        gt[half] = gb[pl.ds(half * QB, QB), :].T
        dqa[half] = jnp.zeros((HD, QB), F32)

    def pass_keys(tile):
        with jax.named_scope("wait_keys"):
            for a, dst in enumerate((kb, vb)):
                arrived(dst.at[pl.ds(0, TILE_SLOTS * ROWS)], k_r.at[a, tile])
        for i in range(TILE_SLOTS):
            for a, dst in enumerate((kb, vb)):
                mine = dst.at[rows_at((tile * TILE_SLOTS + i) * 2 * ROWS + core * ROWS, ROWS)]
                pltpu.make_async_remote_copy(
                    src_ref=mine,
                    dst_ref=mine,
                    send_sem=fw_s.at[a],
                    recv_sem=fw_r.at[a, tile],
                    device_id=partner,
                    device_id_type=MESH,
                ).start()

    def take_keys(tile):
        with jax.named_scope("wait_partner_keys"):
            for a, dst in enumerate((kb, vb)):
                arrived(dst.at[pl.ds(0, TILE_SLOTS * ROWS)], fw_r.at[a, tile])

    def forward(half, tile, stats, start, size, kept=None):
        top, total, dots = stats
        keys = rows_at(start, size)
        rows = kb[keys, :]
        scores = mm(jnp.concatenate([rows, rows], 1), qt[half], 1, 0)
        dprobs = mm(vb[keys, :], gt[half], 1, 0)
        top_new = jnp.maximum(top, jnp.ceil(jnp.max(scores, axis=0, keepdims=True)))
        e = jnp.exp2(scores - top_new)
        shrink = jnp.exp2(top - top_new)
        total = total * shrink + jnp.sum(e, axis=0, keepdims=True)
        dots = dots * shrink + jnp.sum(e * dprobs, axis=0, keepdims=True)
        e_s[half, keys, :] = e.astype(BF16)
        if kept is not None:
            kept[...] = dprobs
        m_s[half, pl.ds(tile, 1), :] = top_new
        return top_new, total, dots

    def end_forward(half, stats):
        top, total, dots = stats
        inverse = 1.0 / total
        gi[half] = (gt[half].astype(F32) * inverse).astype(BF16)
        both = qt[half, :HD].astype(F32) + qt[half, HD:].astype(F32)
        qi[half] = (both * (inverse / LOG2E)).astype(BF16)
        return top, dots * inverse, inverse * SCALE

    def backward(half, tile, stats, start, size, first=False, pair=False, kept=None):
        top, mean, _ = stats
        keys = rows_at(start, size)
        last = m_s[half, pl.ds(tile, 1), :]
        e = e_s[half, keys, :]
        if pair:
            step = jnp.exp2(m_s[half, pl.ds(tile - 1, 1), :] - last).astype(BF16)
            e = jnp.concatenate([e[: size // 2] * step, e[size // 2 :]], 0)
        factor = jnp.exp2(last - top)
        low = factor.astype(BF16)
        part_v = mm(e, gi[half] * low, 1, 1)
        va[keys, :] = part_v if first else va[keys, :] + part_v
        dprobs = mm(vb[keys, :], gt[half], 1, 0) if kept is None else kept[...]
        ds = (e.astype(F32) * (dprobs - mean)).astype(BF16)
        part_k = mm(ds, qi[half] * low, 1, 1)
        ka[keys, :] = part_k if first else ka[keys, :] + part_k
        dqa[half] += mm(kb[keys, :], ds, 0, 0) * factor

    def out_copy(a, src, dst, slot):
        device, _ = chip(slot, -1)
        return pltpu.make_async_remote_copy(
            src_ref=src,
            dst_ref=dst.at[0, :, feat(head)],
            send_sem=out_s.at[a],
            recv_sem=out_r.at[a],
            device_id=device,
            device_id_type=MESH,
        )

    def send_out(a, src, dst, slot):
        def here():
            pltpu.make_async_copy(src, dst.at[0, :, feat(head)], out_r.at[a]).start()

        def there():
            out_copy(a, src, dst, slot).start()

        if isinstance(slot, int):
            there() if slot else here()
        else:
            pl.when(slot > 0)(there)
            pl.when(slot == 0)(here)

    def send_dq(half, stats):
        with jax.named_scope("send_dq"):
            qb[pl.ds(half * QB, QB), :] = (dqa[half] * stats[2]).T.astype(BF16)
            for slot in range(half * HALF_SLOTS, (half + 1) * HALF_SLOTS):
                send_out(0, qb.at[pl.ds(slot * ROWS, ROWS)], dq_o, slot)

    low = jnp.full((1, QB), -1e30, F32)
    zero = jnp.zeros((1, QB), F32)
    start = (low, zero, zero)

    def step_first(tile, stats):
        @pl.when(tile < TILES - 1)
        def _():
            pass_keys(tile + 1)

        @pl.when(tile == 2)
        def _():
            send_q(range(HALF_SLOTS, SLOTS))

        take_keys(tile)
        with jax.named_scope("forward_first"):
            return forward(0, tile, stats, tile * KT, KT, dp_s.at[rows_at(tile * KT, KT)])

    take_queries(0)
    first = forward(0, TILES, start, KEYS, COND, dp_s.at[pl.ds(KEYS, COND)])
    pass_keys(0)
    first = end_forward(0, lax.fori_loop(0, TILES, step_first, first))

    last = BACK_TILES - 1
    with jax.named_scope("backward_first"):
        backward(0, TILES, first, KEYS, COND, True, kept=dp_s.at[pl.ds(KEYS, COND)])
        for tile in (last, last - 1):
            backward(0, 2 * tile + 1, first, tile * BT, BT, True, True, dp_s.at[rows_at(tile * BT, BT)])

    def step_second(tile, stats):
        with jax.named_scope("forward_second"):
            return forward(1, tile, stats, tile * BT, BT)

    def step_kept(tile, stats):
        with jax.named_scope("forward_second"):
            return forward(1, tile, stats, tile * BT, BT, dp_t.at[rows_at((tile - KEPT) * BT, BT)])

    take_queries(1)
    second = forward(1, BACK_TILES, start, KEYS, COND)
    second = lax.fori_loop(0, KEPT, step_second, second)
    second = end_forward(1, lax.fori_loop(KEPT, BACK_TILES, step_kept, second))
    backward(1, BACK_TILES, second, KEYS, COND)

    @pl.when(core == 0)
    def _():
        c_st[...] = va[pl.ds(KEYS, COND), :].astype(BF16)

    @pl.when(core == 1)
    def _():
        c_st[...] = ka[pl.ds(KEYS, COND), :].astype(BF16)

    pltpu.make_async_remote_copy(
        src_ref=c_st, dst_ref=c_rx, send_sem=c1_s, recv_sem=c1_r, device_id=partner, device_id_type=MESH
    ).start()

    def cond_sum():
        arrived(c_rx, c1_r)

        @pl.when(core == 0)
        def _():
            cga[0] = (ka[pl.ds(KEYS, COND), :] + c_rx[...].astype(F32)).astype(BF16)

        @pl.when(core == 1)
        def _():
            cga[0] = (va[pl.ds(KEYS, COND), :] + c_rx[...].astype(F32)).astype(BF16)

        for dz in range(1, 8):
            pltpu.make_async_remote_copy(
                src_ref=cga.at[0],
                dst_ref=cga.at[dz],
                send_sem=cg_s,
                recv_sem=cg_r,
                device_id={"dp": (z + dz) % 8},
                device_id_type=MESH,
            ).start()

    def part_copy(dt):
        owner = (tp + dt) % 4
        return pltpu.make_async_remote_copy(
            src_ref=prod.at[pl.ds(pl.multiple_of((z % 2) * 64 + owner * 112, 16), 112)],
            dst_ref=w_o.at[tp],
            send_sem=w_s,
            recv_sem=w_r,
            device_id={"tp": owner},
            device_id_type=MESH,
        )

    def cond_product():
        arrived(hida.at[pl.ds(1, 7)], hid_r)
        arrived(cga.at[pl.ds(1, 7)], cg_r)
        prod[...] = mm(
            hida[...].reshape(8 * COND, WINDOW), cga[...].reshape(8 * COND, HD), 0, 0
        ).astype(BF16)
        for dt in range(1, 4):
            part_copy(dt).start()
        pltpu.make_async_copy(
            prod.at[pl.ds(pl.multiple_of((z % 2) * 64 + tp * 112, 16), 112)], w_o.at[tp], w_r
        ).start()

    def swap(unit, slot, count):
        for i in range(count):
            theirs = rows_at((slot + i) * 2 * ROWS + (1 - core) * ROWS, ROWS)
            st[0, slot + i] = ka[theirs, :].astype(BF16)
            st[1, slot + i] = va[theirs, :].astype(BF16)
        for a in range(2):
            part = pl.ds(slot, count)
            pltpu.make_async_remote_copy(
                src_ref=st.at[a, part],
                dst_ref=rx.at[a, part],
                send_sem=ex_s.at[a],
                recv_sem=ex_r.at[a, unit],
                device_id=partner,
                device_id_type=MESH,
            ).start()

    def finish(unit, slot, count):
        with jax.named_scope("finish"):
            for a in range(2):
                arrived(rx.at[a, pl.ds(slot, count)], ex_r.at[a, unit])
            for a, (acc, dst) in enumerate(((ka, dk_o), (va, dv_o))):
                for i in range(count):
                    mine = rows_at((slot + i) * 2 * ROWS + core * ROWS, ROWS)
                    rx[a, slot + i] = (acc[mine, :] + rx[a, slot + i].astype(F32)).astype(BF16)
                    send_out(1 + a, rx.at[a, slot + i], dst, slot + i)

    for unit in range(2):
        with jax.named_scope("backward_tile"):
            backward(
                1, last, second, last * BT + unit * KT, KT,
                kept=dp_t.at[pl.ds((last - KEPT) * BT + unit * KT, KT)],
            )
        swap(unit, last * BACK_SLOTS + unit * 2, 2)
    with jax.named_scope("condition_sum"):
        cond_sum()
    finish(0, last * BACK_SLOTS, 2)

    with jax.named_scope("backward_tile"):
        backward(
            1, last - 1, second, (last - 1) * BT, BT, kept=dp_t.at[pl.ds((last - 1 - KEPT) * BT, BT)]
        )
    swap(2, (last - 1) * BACK_SLOTS, BACK_SLOTS)
    finish(1, last * BACK_SLOTS + 2, 2)

    def back(step, carry):
        tile = last - step
        with jax.named_scope("backward_tile"):
            backward(1, tile, second, tile * BT, BT, True)

        @pl.when(tile == 0)
        def _():
            send_dq(1, second)

        @pl.when(tile == 0)
        def _():
            with jax.named_scope("condition_product"):
                cond_product()

        finish(step, (tile + 1) * BACK_SLOTS, BACK_SLOTS)
        with jax.named_scope("backward_tile"):
            backward(0, 2 * tile + 1, first, tile * BT, BT, False, True, dp_s.at[rows_at(tile * BT, BT)])
        swap(step + 1, tile * BACK_SLOTS, BACK_SLOTS)
        return carry

    lax.fori_loop(2, BACK_TILES, back, 0)
    send_dq(0, first)
    finish(BACK_TILES, 0, BACK_SLOTS)

    with jax.named_scope("drain"):
        sent = pl.ds(0, (SLOTS - 1) * ROWS)
        for a in range(4):
            arrived(qb.at[sent], in_s.at[a])
        for a in range(2):
            arrived(qb, fw_s.at[a])
            arrived(st.at[a], ex_s.at[a])
        arrived(c_st, c1_s)
        arrived(hida.at[pl.ds(1, 7)], hid_s)
        arrived(cga.at[pl.ds(1, 7)], cg_s)
        for a in range(3):
            arrived(qb.at[sent], out_s.at[a])
    with jax.named_scope("drain_weight"):
        arrived(w_o.at[pl.ds(0, 3)], w_s)
        arrived(w_o, w_r)
    with jax.named_scope("drain_key"):
        arrived(dk_o.at[0], out_r.at[1])
    with jax.named_scope("drain_value"):
        arrived(dv_o.at[0], out_r.at[2])
    with jax.named_scope("drain_query"):
        arrived(dq_o.at[0], out_r.at[0])


def place(dq, dk, dv, parts, dq_o, dk_o, dv_o, w_o, held, held_w, full_w, in_s, out_s, w_s):
    fetch_w = pltpu.make_async_copy(parts, held_w, w_s.at[0])
    store_w = pltpu.make_async_copy(full_w, w_o, w_s.at[1])
    fetches = [
        pltpu.make_async_copy(src, held.at[a], in_s.at[a]) for a, src in enumerate((dq, dk, dv))
    ]
    stores = [
        pltpu.make_async_copy(held.at[a], dst, out_s.at[a])
        for a, dst in enumerate((dq_o, dk_o, dv_o))
    ]
    fetch_w.start()
    for fetch in fetches:
        fetch.start()
    fetch_w.wait()
    for half in range(2):
        for array in range(2):
            columns = slice(half * HD, (half + 1) * HD)
            full_w[:, array, columns] = held_w[2 * half + array].astype(F32)
    store_w.start()
    for fetch, store in zip(fetches, stores):
        fetch.wait()
        store.start()
    store_w.wait()
    for store in stores:
        store.wait()


def on_device(latent_query, latent_key, latent_value, out_grad, query_hidden, cond_weight):
    anywhere = pl.BlockSpec(memory_space=pl.ANY)
    token = jax.ShapeDtypeStruct(latent_query.shape, BF16)
    dma = pltpu.SemaphoreType.DMA
    total_keys = KEYS + COND
    grads = pl.pallas_call(
        kernel,
        name="attention_backward",
        out_shape=(token, token, token, jax.ShapeDtypeStruct((4, 112, HD), BF16)),
        in_specs=[anywhere] * 6,
        out_specs=(anywhere,) * 4,
        scratch_shapes=[
            pltpu.VMEM((2 * QB, HD), BF16),
            pltpu.VMEM((2 * QB, HD), BF16),
            pltpu.VMEM((total_keys, HD), BF16),
            pltpu.VMEM((total_keys, HD), BF16),
            pltpu.VMEM((2, 2 * HD, QB), BF16),
            pltpu.VMEM((2, HD, QB), BF16),
            pltpu.VMEM((2, HD, QB), BF16),
            pltpu.VMEM((2, HD, QB), BF16),
            pltpu.VMEM((2, total_keys, QB), BF16),
            pltpu.VMEM((total_keys, QB), F32),
            pltpu.VMEM(((BACK_TILES - KEPT) * BT, QB), F32),
            pltpu.VMEM((2, 16, QB), F32),
            pltpu.VMEM((total_keys, HD), F32),
            pltpu.VMEM((total_keys, HD), F32),
            pltpu.VMEM((2, HD, QB), F32),
            pltpu.VMEM((2, SLOTS, ROWS, HD), BF16),
            pltpu.VMEM((2, SLOTS, ROWS, HD), BF16),
            pltpu.VMEM((cond_weight.shape[0], 2, HD), BF16),
            pltpu.VMEM(query_hidden.shape, BF16),
            pltpu.VMEM((8, COND, WINDOW), BF16),
            pltpu.VMEM((COND, HD), BF16),
            pltpu.VMEM((COND, HD), BF16),
            pltpu.VMEM((8, COND, HD), BF16),
            pltpu.VMEM((WINDOW, HD), BF16),
            dma((4,)), dma((2, SLOTS // GROUP)), dma((2, TILES)),
            dma((2,)), dma((2, TILES)),
            dma((2,)), dma((2, BACK_TILES + 1)),
            dma((3,)), dma((3,)),
            dma, dma,
            dma, dma,
            dma, dma,
            dma, dma,
            dma, dma,
        ],
        compiler_params=pltpu.CompilerParams(
            collective_id=0, has_side_effects=True, vmem_limit_bytes=63 << 20
        ),
    )(latent_query, latent_key, latent_value, out_grad, query_hidden, cond_weight)
    weight = jax.ShapeDtypeStruct((112, 2, 2 * HD), F32)
    return pl.pallas_call(
        place,
        name="place_outputs",
        out_shape=(token, token, token, weight),
        in_specs=[anywhere] * 4,
        out_specs=(anywhere,) * 4,
        scratch_shapes=[
            pltpu.VMEM((3,) + latent_query.shape, BF16),
            pltpu.VMEM((4, 112, HD), BF16),
            pltpu.VMEM((112, 2, 2 * HD), F32),
            dma((3,)), dma((3,)), dma((2,)),
        ],
    )(*grads)


def solution(mesh):
    placed = (
        P("dp", ("seq", "tp"), None),
        P("dp", ("seq", "tp"), None),
        P("dp", ("seq", "tp"), None),
        P("dp", ("seq", "tp"), None),
        P("dp", None, None),
        P(None, None, "seq"),
    )
    return jax.shard_map(
        on_device,
        mesh=mesh,
        in_specs=placed,
        out_specs=(
            P("dp", ("seq", "tp"), None),
            P("dp", ("seq", "tp"), None),
            P("dp", ("seq", "tp"), None),
            P(("dp", "tp"), None, "seq"),
        ),
        check_vma=False,
    )
```

```python
import jax
import jax.numpy as jnp
from jax import lax
from jax.experimental import pallas as pl
from jax.experimental.pallas import tpu as pltpu
from jax.sharding import PartitionSpec as P

HD = 128
MESH = pl.DeviceIdType.MESH
F32 = jnp.float32
BF16 = jnp.bfloat16
SCALE = HD ** (-0.5)
LOG2E = 1.4426950408889634
ROWS = 128
SLOTS = 16
HALF_SLOTS = 10
QB = (HALF_SLOTS * ROWS, (SLOTS - HALF_SLOTS) * ROWS)
KT = 512
BT = 2 * KT
KEYS = 4096
COND = 64
TILES = KEYS // KT
TILE_SLOTS = SLOTS // TILES
BACK_TILES = KEYS // BT
BACK_SLOTS = SLOTS // BACK_TILES
KEPT = BACK_TILES - 1
GROUP = 2
WINDOW = 512


def mm(a, b, ca, cb):
    return lax.dot_general(a, b, (((ca,), (cb,)), ((), ())), preferred_element_type=F32)


OFFSETS = (
    (0, 0), (0, 1), (1, 0), (0, 3), (3, 0), (1, 1), (3, 3), (2, 0),
    (0, 2), (1, 3), (3, 1), (1, 2), (2, 1), (3, 2), (2, 3), (2, 2),
)


def pick(slot, values):
    if isinstance(slot, int):
        return values[slot]
    out = values[0]
    for k in range(1, len(values)):
        if values[k] != values[k - 1]:
            out = jnp.where(slot >= k, values[k], out)
    return out


def offset_of(slot):
    return pick(slot, [dx for dx, _ in OFFSETS]), pick(slot, [dy for _, dy in OFFSETS])


def rows_at(start, size):
    if isinstance(start, int):
        return pl.ds(start, size)
    return pl.ds(pl.multiple_of(start, 64), size)


def arrived(ref, sem):
    pltpu.make_async_copy(ref, ref, sem).wait()


def kernel(
    lq, lk, lv, og, hidden, cw,
    dq_o, dk_o, dv_o, w_o,
    qb, gb, kb, vb, qt0, qt1, gt0, gt1, qi0, qi1, gi0, gi1, e0, e1, dp_s, dp_t, m0, m1, ka, va, dqa0, dqa1,
    st, rx, cwv, hid, hida, c_st, c_rx, cga, prod,
    in_s, q_r, k_r, fw_s, fw_r, ex_s, ex_r, out_s, out_r,
    hid_s, hid_r, c1_s, c1_r, cg_s, cg_r, w_s, w_r, cw_sem, hid_sem,
):
    qt, gt, qi, gi = (qt0, qt1), (gt0, gt1), (qi0, qi1), (gi0, gi1)
    e_s, m_s, dqa = (e0, e1), (m0, m1), (dqa0, dqa1)
    z = lax.axis_index("dp")
    seq = lax.axis_index("seq")
    tp = lax.axis_index("tp")
    x = (seq // 4) * 2 + tp // 2
    y = seq % 4
    core = tp % 2
    head = 2 * seq + tp // 2
    partner = {"tp": (tp // 2) * 2 + 1 - core}

    def chip(slot, sign):
        dx, dy = offset_of(slot)
        cx = (x + sign * dx + 4) % 4
        cy = (y + sign * dy + 4) % 4
        cseq = (cx // 2) * 4 + cy
        return {"seq": cseq, "tp": (cx % 2) * 2 + core}, 2 * cseq + cx % 2

    def feat(index):
        return pl.ds(pl.multiple_of(index * HD, HD), HD)

    barrier = pltpu.get_barrier_semaphore()

    for slot in range(1, SLOTS):
        device, _ = chip(slot, 1)
        pl.semaphore_signal(barrier, inc=1, device_id=device, device_id_type=MESH)
    pl.semaphore_signal(barrier, inc=1, device_id=partner, device_id_type=MESH)
    pl.semaphore_signal(barrier, inc=1, device_id={"tp": 3 - tp}, device_id_type=MESH)
    for dz in range(1, 8):
        pl.semaphore_signal(
            barrier, inc=1, device_id={"dp": (z + dz) % 8}, device_id_type=MESH
        )

    weights = pltpu.make_async_copy(
        cw.at[:, :, feat(tp // 2)], cwv, cw_sem
    )
    weights.start()
    rows = pltpu.make_async_copy(hidden, hid, hid_sem)
    rows.start()
    for a, (src, dst) in enumerate(((lq, qb), (og, gb))):
        pltpu.make_async_copy(src.at[0, :, feat(head)], dst.at[pl.ds(0, ROWS)], q_r.at[a, 0]).start()
    for a, (src, dst) in enumerate(((lk, kb), (lv, vb))):
        pltpu.make_async_copy(
            src.at[0, :, feat(head)], dst.at[rows_at(core * ROWS, ROWS)], k_r.at[a, 0]
        ).start()

    with jax.named_scope("barrier"):
        pl.semaphore_wait(barrier, 24)

    def in_copy(a, src, dst, dst_start, slot, arrival):
        device, there = chip(slot, 1)
        return pltpu.make_async_remote_copy(
            src_ref=src.at[0, :, feat(there)],
            dst_ref=dst.at[rows_at(dst_start, ROWS)],
            send_sem=in_s.at[a],
            recv_sem=arrival,
            device_id=device,
            device_id_type=MESH,
        )

    def send_q(slots):
        for slot in slots:
            for a, (src, dst) in enumerate(((lq, qb), (og, gb))):
                in_copy(a, src, dst, slot * ROWS, slot, q_r.at[a, slot // GROUP]).start()

    def send_k(slots):
        for slot in slots:
            row = slot * 2 * ROWS + core * ROWS
            for a, (src, dst) in enumerate(((lk, kb), (lv, vb))):
                in_copy(2 + a, src, dst, row, slot, k_r.at[a, slot // TILE_SLOTS]).start()

    with jax.named_scope("send_inputs"):
        for slot in range(1, SLOTS):
            if slot < HALF_SLOTS:
                send_q([slot])
            send_k([slot])

    def window(zz):
        return pl.ds(pl.multiple_of((7 * zz // 2) * HD, HD), WINDOW)

    rows.wait()
    for dz in range(1, 8):
        there = (z + dz) % 8
        pltpu.make_async_remote_copy(
            src_ref=hid.at[0, :, window(there)],
            dst_ref=hida.at[dz],
            send_sem=hid_s,
            recv_sem=hid_r,
            device_id={"dp": there},
            device_id_type=MESH,
        ).start()
    hida[0] = hid[0, :, window(z)]
    weights.wait()

    def cond_step(i, sums):
        r = pl.multiple_of(i * 512, 512)
        rows = hid[0, :, pl.ds(r, 512)]
        return (
            sums[0] + mm(rows, cwv[pl.ds(r, 512), 0, :], 1, 0),
            sums[1] + mm(rows, cwv[pl.ds(r, 512), 1, :], 1, 0),
        )

    nothing = jnp.zeros((COND, HD), F32)
    with jax.named_scope("condition_keys"):
        cond_k, cond_v = lax.fori_loop(0, 7, cond_step, (nothing, nothing))
    kb[pl.ds(KEYS, COND), :] = cond_k.astype(BF16)
    vb[pl.ds(KEYS, COND), :] = cond_v.astype(BF16)

    def slots_of(half):
        return range(HALF_SLOTS) if half == 0 else range(HALF_SLOTS, SLOTS)

    def rows_of(half):
        return pl.ds(half * QB[0], QB[half])

    def take_queries(half):
        for group in range(slots_of(half)[0] // GROUP, (slots_of(half)[-1] + 1) // GROUP):
            with jax.named_scope("wait_queries"):
                for a, dst in enumerate((qb, gb)):
                    arrived(dst.at[pl.ds(group * GROUP * ROWS, GROUP * ROWS)], q_r.at[a, group])
        scaled = qb[rows_of(half), :].T.astype(F32) * (SCALE * LOG2E)
        high = scaled.astype(BF16)
        qt[half][:HD, :] = high
        qt[half][HD:, :] = (scaled - high.astype(F32)).astype(BF16)
        gt[half][...] = gb[rows_of(half), :].T
        dqa[half][...] = jnp.zeros((HD, QB[half]), F32)

    def pass_keys(tile):
        with jax.named_scope("wait_keys"):
            for a, dst in enumerate((kb, vb)):
                arrived(dst.at[pl.ds(0, TILE_SLOTS * ROWS)], k_r.at[a, tile])
        for i in range(TILE_SLOTS):
            for a, dst in enumerate((kb, vb)):
                mine = dst.at[rows_at((tile * TILE_SLOTS + i) * 2 * ROWS + core * ROWS, ROWS)]
                pltpu.make_async_remote_copy(
                    src_ref=mine,
                    dst_ref=mine,
                    send_sem=fw_s.at[a],
                    recv_sem=fw_r.at[a, tile],
                    device_id=partner,
                    device_id_type=MESH,
                ).start()

    def take_keys(tile):
        with jax.named_scope("wait_partner_keys"):
            for a, dst in enumerate((kb, vb)):
                arrived(dst.at[pl.ds(0, TILE_SLOTS * ROWS)], fw_r.at[a, tile])

    def forward(half, tile, stats, start, size, kept=None):
        top, total, dots = stats
        keys = rows_at(start, size)
        rows = kb[keys, :]
        scores = mm(jnp.concatenate([rows, rows], 1), qt[half][...], 1, 0)
        dprobs = mm(vb[keys, :], gt[half][...], 1, 0)
        top_new = jnp.maximum(top, jnp.ceil(jnp.max(scores, axis=0, keepdims=True)))
        e = jnp.exp2(scores - top_new)
        shrink = jnp.exp2(top - top_new)
        total = total * shrink + jnp.sum(e, axis=0, keepdims=True)
        dots = dots * shrink + jnp.sum(e * dprobs, axis=0, keepdims=True)
        e_s[half][keys, :] = e.astype(BF16)
        if kept is not None:
            kept[...] = dprobs
        m_s[half][pl.ds(tile, 1), :] = top_new
        return top_new, total, dots

    def end_forward(half, stats):
        top, total, dots = stats
        inverse = 1.0 / total
        gi[half][...] = (gt[half][...].astype(F32) * inverse).astype(BF16)
        both = qt[half][:HD, :].astype(F32) + qt[half][HD:, :].astype(F32)
        qi[half][...] = (both * (inverse / LOG2E)).astype(BF16)
        return top, dots * inverse, inverse * SCALE

    def backward(half, tile, stats, start, size, first=False, pair=False, kept=None):
        top, mean, _ = stats
        keys = rows_at(start, size)
        last = m_s[half][pl.ds(tile, 1), :]
        e = e_s[half][keys, :]
        if pair:
            step = jnp.exp2(m_s[half][pl.ds(tile - 1, 1), :] - last).astype(BF16)
            e = jnp.concatenate([e[: size // 2] * step, e[size // 2 :]], 0)
        factor = jnp.exp2(last - top)
        low = factor.astype(BF16)
        part_v = mm(e, gi[half][...] * low, 1, 1)
        va[keys, :] = part_v if first else va[keys, :] + part_v
        dprobs = mm(vb[keys, :], gt[half][...], 1, 0) if kept is None else kept[...]
        ds = (e.astype(F32) * (dprobs - mean)).astype(BF16)
        part_k = mm(ds, qi[half][...] * low, 1, 1)
        ka[keys, :] = part_k if first else ka[keys, :] + part_k
        dqa[half][...] += mm(kb[keys, :], ds, 0, 0) * factor

    def out_copy(a, src, dst, slot):
        device, _ = chip(slot, -1)
        return pltpu.make_async_remote_copy(
            src_ref=src,
            dst_ref=dst.at[0, :, feat(head)],
            send_sem=out_s.at[a],
            recv_sem=out_r.at[a],
            device_id=device,
            device_id_type=MESH,
        )

    def send_out(a, src, dst, slot):
        def here():
            pltpu.make_async_copy(src, dst.at[0, :, feat(head)], out_r.at[a]).start()

        def there():
            out_copy(a, src, dst, slot).start()

        if isinstance(slot, int):
            there() if slot else here()
        else:
            pl.when(slot > 0)(there)
            pl.when(slot == 0)(here)

    def send_dq(half, stats):
        with jax.named_scope("send_dq"):
            qb[rows_of(half), :] = (dqa[half][...] * stats[2]).T.astype(BF16)
            for slot in slots_of(half):
                send_out(0, qb.at[pl.ds(slot * ROWS, ROWS)], dq_o, slot)

    def start(half):
        zero = jnp.zeros((1, QB[half]), F32)
        return zero - 1e30, zero, zero

    def step_first(tile, stats):
        @pl.when(tile < TILES - 1)
        def _():
            pass_keys(tile + 1)

        @pl.when(tile == 2)
        def _():
            send_q(range(HALF_SLOTS, SLOTS))

        take_keys(tile)
        with jax.named_scope("forward_first"):
            return forward(0, tile, stats, tile * KT, KT, dp_s.at[rows_at(tile * KT, KT)])

    take_queries(0)
    first = forward(0, TILES, start(0), KEYS, COND, dp_s.at[pl.ds(KEYS, COND)])
    pass_keys(0)
    first = end_forward(0, lax.fori_loop(0, TILES, step_first, first))

    last = BACK_TILES - 1
    with jax.named_scope("backward_first"):
        backward(0, TILES, first, KEYS, COND, True, kept=dp_s.at[pl.ds(KEYS, COND)])
        for tile in (last, last - 1):
            backward(0, 2 * tile + 1, first, tile * BT, BT, True, True, dp_s.at[rows_at(tile * BT, BT)])

    def step_second(tile, stats):
        with jax.named_scope("forward_second"):
            return forward(1, tile, stats, tile * BT, BT)

    def step_kept(tile, stats):
        with jax.named_scope("forward_second"):
            return forward(1, tile, stats, tile * BT, BT, dp_t.at[rows_at((tile - KEPT) * BT, BT)])

    take_queries(1)
    second = forward(1, BACK_TILES, start(1), KEYS, COND)
    second = lax.fori_loop(0, KEPT, step_second, second)
    second = end_forward(1, lax.fori_loop(KEPT, BACK_TILES, step_kept, second))

    def cond_sum():
        arrived(c_rx, c1_r)

        @pl.when(core == 0)
        def _():
            cga[0] = (ka[pl.ds(KEYS, COND), :] + c_rx[...].astype(F32)).astype(BF16)

        @pl.when(core == 1)
        def _():
            cga[0] = (va[pl.ds(KEYS, COND), :] + c_rx[...].astype(F32)).astype(BF16)

        for dz in range(1, 8):
            pltpu.make_async_remote_copy(
                src_ref=cga.at[0],
                dst_ref=cga.at[dz],
                send_sem=cg_s,
                recv_sem=cg_r,
                device_id={"dp": (z + dz) % 8},
                device_id_type=MESH,
            ).start()

    def part_copy(dt):
        owner = (tp + dt) % 4
        return pltpu.make_async_remote_copy(
            src_ref=prod.at[pl.ds(pl.multiple_of((z % 2) * 64 + owner * 112, 16), 112)],
            dst_ref=w_o.at[tp],
            send_sem=w_s,
            recv_sem=w_r,
            device_id={"tp": owner},
            device_id_type=MESH,
        )

    def cond_product():
        arrived(hida.at[pl.ds(1, 7)], hid_r)
        arrived(cga.at[pl.ds(1, 7)], cg_r)
        prod[...] = mm(
            hida[...].reshape(8 * COND, WINDOW), cga[...].reshape(8 * COND, HD), 0, 0
        ).astype(BF16)
        for dt in range(1, 4):
            part_copy(dt).start()
        pltpu.make_async_copy(
            prod.at[pl.ds(pl.multiple_of((z % 2) * 64 + tp * 112, 16), 112)], w_o.at[tp], w_r
        ).start()

    def swap(unit, slot, count):
        for i in range(count):
            theirs = rows_at((slot + i) * 2 * ROWS + (1 - core) * ROWS, ROWS)
            st[0, slot + i] = ka[theirs, :].astype(BF16)
            st[1, slot + i] = va[theirs, :].astype(BF16)
        for a in range(2):
            part = pl.ds(slot, count)
            pltpu.make_async_remote_copy(
                src_ref=st.at[a, part],
                dst_ref=rx.at[a, part],
                send_sem=ex_s.at[a],
                recv_sem=ex_r.at[a, unit],
                device_id=partner,
                device_id_type=MESH,
            ).start()

    def finish(unit, slot, count):
        with jax.named_scope("finish"):
            for a in range(2):
                arrived(rx.at[a, pl.ds(slot, count)], ex_r.at[a, unit])
            for a, (acc, dst) in enumerate(((ka, dk_o), (va, dv_o))):
                for i in range(count):
                    mine = rows_at((slot + i) * 2 * ROWS + core * ROWS, ROWS)
                    rx[a, slot + i] = (acc[mine, :] + rx[a, slot + i].astype(F32)).astype(BF16)
                    send_out(1 + a, rx.at[a, slot + i], dst, slot + i)

    def first_tile(unit):
        with jax.named_scope("backward_tile"):
            backward(
                1, last, second, last * BT + unit * KT, KT,
                kept=dp_t.at[pl.ds((last - KEPT) * BT + unit * KT, KT)],
            )
        swap(unit, last * BACK_SLOTS + unit * 2, 2)

    first_tile(0)
    backward(1, BACK_TILES, second, KEYS, COND)

    @pl.when(core == 0)
    def _():
        c_st[...] = va[pl.ds(KEYS, COND), :].astype(BF16)

    @pl.when(core == 1)
    def _():
        c_st[...] = ka[pl.ds(KEYS, COND), :].astype(BF16)

    pltpu.make_async_remote_copy(
        src_ref=c_st, dst_ref=c_rx, send_sem=c1_s, recv_sem=c1_r, device_id=partner, device_id_type=MESH
    ).start()

    first_tile(1)
    finish(0, last * BACK_SLOTS, 2)
    with jax.named_scope("condition_sum"):
        cond_sum()

    with jax.named_scope("backward_tile"):
        backward(1, last - 1, second, (last - 1) * BT, BT)
    swap(2, (last - 1) * BACK_SLOTS, BACK_SLOTS)
    finish(1, last * BACK_SLOTS + 2, 2)

    def back(step, carry):
        tile = last - step
        with jax.named_scope("backward_tile"):
            backward(1, tile, second, tile * BT, BT, True)

        @pl.when(tile == 0)
        def _():
            send_dq(1, second)

        @pl.when(tile == 0)
        def _():
            with jax.named_scope("condition_product"):
                cond_product()

        finish(step, (tile + 1) * BACK_SLOTS, BACK_SLOTS)
        with jax.named_scope("backward_tile"):
            backward(0, 2 * tile + 1, first, tile * BT, BT, False, True, dp_s.at[rows_at(tile * BT, BT)])
        swap(step + 1, tile * BACK_SLOTS, BACK_SLOTS)
        return carry

    lax.fori_loop(2, BACK_TILES, back, 0)
    send_dq(0, first)
    finish(BACK_TILES, 0, BACK_SLOTS)

    with jax.named_scope("drain"):
        sent = pl.ds(0, (SLOTS - 1) * ROWS)
        for a in range(4):
            arrived(qb.at[sent], in_s.at[a])
        for a in range(2):
            arrived(qb, fw_s.at[a])
            arrived(st.at[a], ex_s.at[a])
        arrived(c_st, c1_s)
        arrived(hida.at[pl.ds(1, 7)], hid_s)
        arrived(cga.at[pl.ds(1, 7)], cg_s)
        for a in range(3):
            arrived(qb.at[sent], out_s.at[a])
    with jax.named_scope("drain_weight"):
        arrived(w_o.at[pl.ds(0, 3)], w_s)
        arrived(w_o, w_r)
    with jax.named_scope("drain_key"):
        arrived(dk_o.at[0], out_r.at[1])
    with jax.named_scope("drain_value"):
        arrived(dv_o.at[0], out_r.at[2])
    with jax.named_scope("drain_query"):
        arrived(dq_o.at[0], out_r.at[0])


def place(dq, dk, dv, parts, dq_o, dk_o, dv_o, w_o, held, held_w, full_w, in_s, out_s, w_s):
    fetch_w = pltpu.make_async_copy(parts, held_w, w_s.at[0])
    store_w = pltpu.make_async_copy(full_w, w_o, w_s.at[1])
    fetches = [
        pltpu.make_async_copy(src, held.at[a], in_s.at[a]) for a, src in enumerate((dq, dk, dv))
    ]
    stores = [
        pltpu.make_async_copy(held.at[a], dst, out_s.at[a])
        for a, dst in enumerate((dq_o, dk_o, dv_o))
    ]
    fetch_w.start()
    for fetch in fetches:
        fetch.start()
    fetch_w.wait()
    for half in range(2):
        for array in range(2):
            columns = slice(half * HD, (half + 1) * HD)
            full_w[:, array, columns] = held_w[2 * half + array].astype(F32)
    store_w.start()
    for fetch, store in zip(fetches, stores):
        fetch.wait()
        store.start()
    store_w.wait()
    for store in stores:
        store.wait()


def on_device(latent_query, latent_key, latent_value, out_grad, query_hidden, cond_weight):
    anywhere = pl.BlockSpec(memory_space=pl.ANY)
    token = jax.ShapeDtypeStruct(latent_query.shape, BF16)
    dma = pltpu.SemaphoreType.DMA
    total_keys = KEYS + COND
    grads = pl.pallas_call(
        kernel,
        name="attention_backward",
        out_shape=(token, token, token, jax.ShapeDtypeStruct((4, 112, HD), BF16)),
        in_specs=[anywhere] * 6,
        out_specs=(anywhere,) * 4,
        scratch_shapes=[
            pltpu.VMEM((SLOTS * ROWS, HD), BF16),
            pltpu.VMEM((SLOTS * ROWS, HD), BF16),
            pltpu.VMEM((total_keys, HD), BF16),
            pltpu.VMEM((total_keys, HD), BF16),
            *(pltpu.VMEM((2 * HD, n), BF16) for n in QB),
            *(pltpu.VMEM((HD, n), BF16) for n in QB * 3),
            *(pltpu.VMEM((total_keys, n), BF16) for n in QB),
            pltpu.VMEM((total_keys, QB[0]), F32),
            pltpu.VMEM(((BACK_TILES - KEPT) * BT, QB[1]), F32),
            *(pltpu.VMEM((16, n), F32) for n in QB),
            pltpu.VMEM((total_keys, HD), F32),
            pltpu.VMEM((total_keys, HD), F32),
            *(pltpu.VMEM((HD, n), F32) for n in QB),
            pltpu.VMEM((2, SLOTS, ROWS, HD), BF16),
            pltpu.VMEM((2, SLOTS, ROWS, HD), BF16),
            pltpu.VMEM((cond_weight.shape[0], 2, HD), BF16),
            pltpu.VMEM(query_hidden.shape, BF16),
            pltpu.VMEM((8, COND, WINDOW), BF16),
            pltpu.VMEM((COND, HD), BF16),
            pltpu.VMEM((COND, HD), BF16),
            pltpu.VMEM((8, COND, HD), BF16),
            pltpu.VMEM((WINDOW, HD), BF16),
            dma((4,)), dma((2, SLOTS // GROUP)), dma((2, TILES)),
            dma((2,)), dma((2, TILES)),
            dma((2,)), dma((2, BACK_TILES + 1)),
            dma((3,)), dma((3,)),
            dma, dma,
            dma, dma,
            dma, dma,
            dma, dma,
            dma, dma,
        ],
        compiler_params=pltpu.CompilerParams(
            collective_id=0, has_side_effects=True, vmem_limit_bytes=63 << 20
        ),
    )(latent_query, latent_key, latent_value, out_grad, query_hidden, cond_weight)
    weight = jax.ShapeDtypeStruct((112, 2, 2 * HD), F32)
    return pl.pallas_call(
        place,
        name="place_outputs",
        out_shape=(token, token, token, weight),
        in_specs=[anywhere] * 4,
        out_specs=(anywhere,) * 4,
        scratch_shapes=[
            pltpu.VMEM((3,) + latent_query.shape, BF16),
            pltpu.VMEM((4, 112, HD), BF16),
            pltpu.VMEM((112, 2, 2 * HD), F32),
            dma((3,)), dma((3,)), dma((2,)),
        ],
    )(*grads)


def solution(mesh):
    placed = (
        P("dp", ("seq", "tp"), None),
        P("dp", ("seq", "tp"), None),
        P("dp", ("seq", "tp"), None),
        P("dp", ("seq", "tp"), None),
        P("dp", None, None),
        P(None, None, "seq"),
    )
    return jax.shard_map(
        on_device,
        mesh=mesh,
        in_specs=placed,
        out_specs=(
            P("dp", ("seq", "tp"), None),
            P("dp", ("seq", "tp"), None),
            P("dp", ("seq", "tp"), None),
            P(("dp", "tp"), None, "seq"),
        ),
        check_vma=False,
    )
```

```python
import jax
import jax.numpy as jnp
from jax import lax
from jax.experimental import pallas as pl
from jax.experimental.pallas import tpu as pltpu
from jax.sharding import PartitionSpec as P

HD = 128
MESH = pl.DeviceIdType.MESH
F32 = jnp.float32
BF16 = jnp.bfloat16
SCALE = HD ** (-0.5)
LOG2E = 1.4426950408889634
ROWS = 128
SLOTS = 16
HALF_SLOTS = 10
QB = (HALF_SLOTS * ROWS, (SLOTS - HALF_SLOTS) * ROWS)
KT = 512
BT = 2 * KT
KEYS = 4096
COND = 64
TILES = KEYS // KT
TILE_SLOTS = SLOTS // TILES
BACK_TILES = KEYS // BT
BACK_SLOTS = SLOTS // BACK_TILES
KEPT = BACK_TILES - 1
GROUP = 2
WINDOW = 512


def mm(a, b, ca, cb):
    return lax.dot_general(a, b, (((ca,), (cb,)), ((), ())), preferred_element_type=F32)


OFFSETS = (
    (0, 0), (0, 1), (1, 0), (0, 3), (3, 0), (1, 1), (3, 3), (2, 0),
    (0, 2), (1, 3), (3, 1), (1, 2), (2, 1), (3, 2), (2, 3), (2, 2),
)


def pick(slot, values):
    if isinstance(slot, int):
        return values[slot]
    out = values[0]
    for k in range(1, len(values)):
        if values[k] != values[k - 1]:
            out = jnp.where(slot >= k, values[k], out)
    return out


def offset_of(slot):
    return pick(slot, [dx for dx, _ in OFFSETS]), pick(slot, [dy for _, dy in OFFSETS])


def rows_at(start, size):
    if isinstance(start, int):
        return pl.ds(start, size)
    return pl.ds(pl.multiple_of(start, 64), size)


def arrived(ref, sem):
    pltpu.make_async_copy(ref, ref, sem).wait()


def kernel(
    lq, lk, lv, og, hidden, cw,
    dq_o, dk_o, dv_o, w_o,
    qb, gb, kb, vb, qt0, qt1, gt0, gt1, qi0, qi1, gi0, gi1, e0, e1, dp_s, dp_t, m0, m1, ka, va, dqa0, dqa1,
    st, rx, cwv, hid, hida, c_st, c_rx, cga, prod,
    in_s, q_r, k_r, fw_s, fw_r, ex_s, ex_r, out_s, out_r,
    hid_s, hid_r, c1_s, c1_r, cg_s, cg_r, w_s, w_r, cw_sem, hid_sem,
):
    qt, gt, qi, gi = (qt0, qt1), (gt0, gt1), (qi0, qi1), (gi0, gi1)
    e_s, m_s, dqa = (e0, e1), (m0, m1), (dqa0, dqa1)
    z = lax.axis_index("dp")
    seq = lax.axis_index("seq")
    tp = lax.axis_index("tp")
    x = (seq // 4) * 2 + tp // 2
    y = seq % 4
    core = tp % 2
    head = 2 * seq + tp // 2
    partner = {"tp": (tp // 2) * 2 + 1 - core}

    def chip(slot, sign):
        dx, dy = offset_of(slot)
        cx = (x + sign * dx + 4) % 4
        cy = (y + sign * dy + 4) % 4
        cseq = (cx // 2) * 4 + cy
        return {"seq": cseq, "tp": (cx % 2) * 2 + core}, 2 * cseq + cx % 2

    def feat(index):
        return pl.ds(pl.multiple_of(index * HD, HD), HD)

    barrier = pltpu.get_barrier_semaphore()

    for slot in range(1, SLOTS):
        device, _ = chip(slot, 1)
        pl.semaphore_signal(barrier, inc=1, device_id=device, device_id_type=MESH)
    pl.semaphore_signal(barrier, inc=1, device_id=partner, device_id_type=MESH)
    pl.semaphore_signal(barrier, inc=1, device_id={"tp": 3 - tp}, device_id_type=MESH)
    for dz in range(1, 8):
        pl.semaphore_signal(
            barrier, inc=1, device_id={"dp": (z + dz) % 8}, device_id_type=MESH
        )

    weights = pltpu.make_async_copy(
        cw.at[:, :, feat(tp // 2)], cwv, cw_sem
    )
    weights.start()
    rows = pltpu.make_async_copy(hidden, hid, hid_sem)
    rows.start()
    for a, (src, dst) in enumerate(((lq, qb), (og, gb))):
        pltpu.make_async_copy(src.at[0, :, feat(head)], dst.at[pl.ds(0, ROWS)], q_r.at[a, 0]).start()
    for a, (src, dst) in enumerate(((lk, kb), (lv, vb))):
        pltpu.make_async_copy(
            src.at[0, :, feat(head)], dst.at[rows_at(core * ROWS, ROWS)], k_r.at[0]
        ).start()

    with jax.named_scope("barrier"):
        pl.semaphore_wait(barrier, 24)

    def in_copy(a, src, dst, dst_start, slot, arrival):
        device, there = chip(slot, 1)
        return pltpu.make_async_remote_copy(
            src_ref=src.at[0, :, feat(there)],
            dst_ref=dst.at[rows_at(dst_start, ROWS)],
            send_sem=in_s.at[a],
            recv_sem=arrival,
            device_id=device,
            device_id_type=MESH,
        )

    def send_q(slots):
        for slot in slots:
            for a, (src, dst) in enumerate(((lq, qb), (og, gb))):
                in_copy(a, src, dst, slot * ROWS, slot, q_r.at[a, slot // HALF_SLOTS]).start()

    def send_k(slots):
        for slot in slots:
            row = slot * 2 * ROWS + core * ROWS
            for a, (src, dst) in enumerate(((lk, kb), (lv, vb))):
                in_copy(2 + a, src, dst, row, slot, k_r.at[slot // TILE_SLOTS]).start()

    with jax.named_scope("send_inputs"):
        for slot in range(1, SLOTS):
            if slot < HALF_SLOTS:
                send_q([slot])
            send_k([slot])

    def window(zz):
        return pl.ds(pl.multiple_of((7 * zz // 2) * HD, HD), WINDOW)

    rows.wait()
    for dz in range(1, 8):
        there = (z + dz) % 8
        pltpu.make_async_remote_copy(
            src_ref=hid.at[0, :, window(there)],
            dst_ref=hida.at[dz],
            send_sem=hid_s,
            recv_sem=hid_r,
            device_id={"dp": there},
            device_id_type=MESH,
        ).start()
    hida[0] = hid[0, :, window(z)]
    weights.wait()

    def cond_step(i, sums):
        r = pl.multiple_of(i * 512, 512)
        rows = hid[0, :, pl.ds(r, 512)]
        return (
            sums[0] + mm(rows, cwv[pl.ds(r, 512), 0, :], 1, 0),
            sums[1] + mm(rows, cwv[pl.ds(r, 512), 1, :], 1, 0),
        )

    nothing = jnp.zeros((COND, HD), F32)
    with jax.named_scope("condition_keys"):
        cond_k, cond_v = lax.fori_loop(0, 7, cond_step, (nothing, nothing))
    kb[pl.ds(KEYS, COND), :] = cond_k.astype(BF16)
    vb[pl.ds(KEYS, COND), :] = cond_v.astype(BF16)

    def slots_of(half):
        return range(HALF_SLOTS) if half == 0 else range(HALF_SLOTS, SLOTS)

    def rows_of(half):
        return pl.ds(half * QB[0], QB[half])

    def take_queries(half):
        with jax.named_scope("wait_queries"):
            for a, dst in enumerate((qb, gb)):
                arrived(dst.at[rows_of(half)], q_r.at[a, half])
        scaled = qb[rows_of(half), :].T.astype(F32) * (SCALE * LOG2E)
        high = scaled.astype(BF16)
        qt[half][:HD, :] = high
        qt[half][HD:, :] = (scaled - high.astype(F32)).astype(BF16)
        gt[half][...] = gb[rows_of(half), :].T
        dqa[half][...] = jnp.zeros((HD, QB[half]), F32)

    def pass_keys(tile):
        with jax.named_scope("wait_keys"):
            arrived(kb.at[pl.ds(0, 2 * TILE_SLOTS * ROWS)], k_r.at[tile])
        for i in range(TILE_SLOTS):
            for a, dst in enumerate((kb, vb)):
                mine = dst.at[rows_at((tile * TILE_SLOTS + i) * 2 * ROWS + core * ROWS, ROWS)]
                pltpu.make_async_remote_copy(
                    src_ref=mine,
                    dst_ref=mine,
                    send_sem=fw_s.at[a],
                    recv_sem=fw_r.at[tile],
                    device_id=partner,
                    device_id_type=MESH,
                ).start()

    def take_keys(tile):
        with jax.named_scope("wait_partner_keys"):
            arrived(kb.at[pl.ds(0, 2 * TILE_SLOTS * ROWS)], fw_r.at[tile])

    def forward(half, tile, stats, start, size, kept=None):
        top, total, dots = stats
        keys = rows_at(start, size)
        rows = kb[keys, :]
        scores = mm(jnp.concatenate([rows, rows], 1), qt[half][...], 1, 0)
        dprobs = mm(vb[keys, :], gt[half][...], 1, 0)
        top_new = jnp.maximum(top, jnp.ceil(jnp.max(scores, axis=0, keepdims=True)))
        e = jnp.exp2(scores - top_new)
        shrink = jnp.exp2(top - top_new)
        total = total * shrink + jnp.sum(e, axis=0, keepdims=True)
        dots = dots * shrink + jnp.sum(e * dprobs, axis=0, keepdims=True)
        e_s[half][keys, :] = e.astype(BF16)
        if kept is not None:
            kept[...] = dprobs
        m_s[half][pl.ds(tile, 1), :] = top_new
        return top_new, total, dots

    def end_forward(half, stats):
        top, total, dots = stats
        inverse = 1.0 / total
        gi[half][...] = (gt[half][...].astype(F32) * inverse).astype(BF16)
        both = qt[half][:HD, :].astype(F32) + qt[half][HD:, :].astype(F32)
        qi[half][...] = (both * (inverse / LOG2E)).astype(BF16)
        return top, dots * inverse, inverse * SCALE

    def backward(half, tile, stats, start, size, first=False, pair=False, kept=None):
        top, mean, _ = stats
        keys = rows_at(start, size)
        last = m_s[half][pl.ds(tile, 1), :]
        e = e_s[half][keys, :]
        if pair:
            step = jnp.exp2(m_s[half][pl.ds(tile - 1, 1), :] - last).astype(BF16)
            e = jnp.concatenate([e[: size // 2] * step, e[size // 2 :]], 0)
        factor = jnp.exp2(last - top)
        low = factor.astype(BF16)
        part_v = mm(e, gi[half][...] * low, 1, 1)
        va[keys, :] = part_v if first else va[keys, :] + part_v
        dprobs = mm(vb[keys, :], gt[half][...], 1, 0) if kept is None else kept[...]
        ds = (e.astype(F32) * (dprobs - mean)).astype(BF16)
        part_k = mm(ds, qi[half][...] * low, 1, 1)
        ka[keys, :] = part_k if first else ka[keys, :] + part_k
        dqa[half][...] += mm(kb[keys, :], ds, 0, 0) * factor

    def out_copy(a, src, dst, slot):
        device, _ = chip(slot, -1)
        return pltpu.make_async_remote_copy(
            src_ref=src,
            dst_ref=dst.at[0, :, feat(head)],
            send_sem=out_s.at[a],
            recv_sem=out_r.at[a],
            device_id=device,
            device_id_type=MESH,
        )

    def send_out(a, src, dst, slot):
        def here():
            pltpu.make_async_copy(src, dst.at[0, :, feat(head)], out_r.at[a]).start()

        def there():
            out_copy(a, src, dst, slot).start()

        if isinstance(slot, int):
            there() if slot else here()
        else:
            pl.when(slot > 0)(there)
            pl.when(slot == 0)(here)

    def send_dq(half, stats):
        with jax.named_scope("send_dq"):
            qb[rows_of(half), :] = (dqa[half][...] * stats[2]).T.astype(BF16)
            for slot in slots_of(half):
                send_out(0, qb.at[pl.ds(slot * ROWS, ROWS)], dq_o, slot)

    def start(half):
        zero = jnp.zeros((1, QB[half]), F32)
        return zero - 1e30, zero, zero

    def step_first(tile, stats):
        @pl.when(tile < TILES - 1)
        def _():
            pass_keys(tile + 1)

        @pl.when(tile == 2)
        def _():
            send_q(range(HALF_SLOTS, SLOTS))

        take_keys(tile)
        with jax.named_scope("forward_first"):
            return forward(0, tile, stats, tile * KT, KT, dp_s.at[rows_at(tile * KT, KT)])

    take_queries(0)
    first = forward(0, TILES, start(0), KEYS, COND, dp_s.at[pl.ds(KEYS, COND)])
    pass_keys(0)
    first = end_forward(0, lax.fori_loop(0, TILES, step_first, first))

    last = BACK_TILES - 1
    with jax.named_scope("backward_first"):
        backward(0, TILES, first, KEYS, COND, True, kept=dp_s.at[pl.ds(KEYS, COND)])
        for tile in (last, last - 1):
            backward(0, 2 * tile + 1, first, tile * BT, BT, True, True, dp_s.at[rows_at(tile * BT, BT)])

    def step_second(tile, stats):
        with jax.named_scope("forward_second"):
            return forward(1, tile, stats, tile * BT, BT)

    def step_kept(tile, stats):
        with jax.named_scope("forward_second"):
            return forward(1, tile, stats, tile * BT, BT, dp_t.at[rows_at((tile - KEPT) * BT, BT)])

    take_queries(1)
    second = forward(1, BACK_TILES, start(1), KEYS, COND)
    second = lax.fori_loop(0, KEPT, step_second, second)
    second = end_forward(1, lax.fori_loop(KEPT, BACK_TILES, step_kept, second))

    def cond_sum():
        arrived(c_rx, c1_r)

        @pl.when(core == 0)
        def _():
            cga[0] = (ka[pl.ds(KEYS, COND), :] + c_rx[...].astype(F32)).astype(BF16)

        @pl.when(core == 1)
        def _():
            cga[0] = (va[pl.ds(KEYS, COND), :] + c_rx[...].astype(F32)).astype(BF16)

        for dz in range(1, 8):
            pltpu.make_async_remote_copy(
                src_ref=cga.at[0],
                dst_ref=cga.at[dz],
                send_sem=cg_s,
                recv_sem=cg_r,
                device_id={"dp": (z + dz) % 8},
                device_id_type=MESH,
            ).start()

    def part_copy(dt):
        owner = (tp + dt) % 4
        return pltpu.make_async_remote_copy(
            src_ref=prod.at[pl.ds(pl.multiple_of((z % 2) * 64 + owner * 112, 16), 112)],
            dst_ref=w_o.at[tp],
            send_sem=w_s,
            recv_sem=w_r,
            device_id={"tp": owner},
            device_id_type=MESH,
        )

    def cond_product():
        arrived(hida.at[pl.ds(1, 7)], hid_r)
        arrived(cga.at[pl.ds(1, 7)], cg_r)
        prod[...] = mm(
            hida[...].reshape(8 * COND, WINDOW), cga[...].reshape(8 * COND, HD), 0, 0
        ).astype(BF16)
        for dt in range(1, 4):
            part_copy(dt).start()
        pltpu.make_async_copy(
            prod.at[pl.ds(pl.multiple_of((z % 2) * 64 + tp * 112, 16), 112)], w_o.at[tp], w_r
        ).start()

    def swap(unit, slot, count):
        for i in range(count):
            theirs = rows_at((slot + i) * 2 * ROWS + (1 - core) * ROWS, ROWS)
            st[0, slot + i] = ka[theirs, :].astype(BF16)
            st[1, slot + i] = va[theirs, :].astype(BF16)
        for a in range(2):
            part = pl.ds(slot, count)
            pltpu.make_async_remote_copy(
                src_ref=st.at[a, part],
                dst_ref=rx.at[a, part],
                send_sem=ex_s.at[a],
                recv_sem=ex_r.at[a, unit],
                device_id=partner,
                device_id_type=MESH,
            ).start()

    def finish(unit, slot, count):
        with jax.named_scope("finish"):
            for a in range(2):
                arrived(rx.at[a, pl.ds(slot, count)], ex_r.at[a, unit])
            for a, (acc, dst) in enumerate(((ka, dk_o), (va, dv_o))):
                for i in range(count):
                    mine = rows_at((slot + i) * 2 * ROWS + core * ROWS, ROWS)
                    rx[a, slot + i] = (acc[mine, :] + rx[a, slot + i].astype(F32)).astype(BF16)
                    send_out(1 + a, rx.at[a, slot + i], dst, slot + i)

    def first_tile(unit):
        with jax.named_scope("backward_tile"):
            backward(
                1, last, second, last * BT + unit * KT, KT,
                kept=dp_t.at[pl.ds((last - KEPT) * BT + unit * KT, KT)],
            )
        swap(unit, last * BACK_SLOTS + unit * 2, 2)

    first_tile(0)
    backward(1, BACK_TILES, second, KEYS, COND)

    @pl.when(core == 0)
    def _():
        c_st[...] = va[pl.ds(KEYS, COND), :].astype(BF16)

    @pl.when(core == 1)
    def _():
        c_st[...] = ka[pl.ds(KEYS, COND), :].astype(BF16)

    pltpu.make_async_remote_copy(
        src_ref=c_st, dst_ref=c_rx, send_sem=c1_s, recv_sem=c1_r, device_id=partner, device_id_type=MESH
    ).start()

    first_tile(1)
    finish(0, last * BACK_SLOTS, 2)
    with jax.named_scope("condition_sum"):
        cond_sum()

    with jax.named_scope("backward_tile"):
        backward(1, last - 1, second, (last - 1) * BT, BT)
    swap(2, (last - 1) * BACK_SLOTS, BACK_SLOTS)
    finish(1, last * BACK_SLOTS + 2, 2)

    def back(step, carry):
        tile = last - step
        with jax.named_scope("backward_tile"):
            backward(1, tile, second, tile * BT, BT, True)

        @pl.when(tile == 0)
        def _():
            send_dq(1, second)

        @pl.when(tile == 0)
        def _():
            with jax.named_scope("condition_product"):
                cond_product()

        finish(step, (tile + 1) * BACK_SLOTS, BACK_SLOTS)
        with jax.named_scope("backward_tile"):
            backward(0, 2 * tile + 1, first, tile * BT, BT, False, True, dp_s.at[rows_at(tile * BT, BT)])
        swap(step + 1, tile * BACK_SLOTS, BACK_SLOTS)
        return carry

    lax.fori_loop(2, BACK_TILES, back, 0)
    send_dq(0, first)
    finish(BACK_TILES, 0, BACK_SLOTS)

    with jax.named_scope("drain"):
        sent = pl.ds(0, (SLOTS - 1) * ROWS)
        for a in range(4):
            arrived(qb.at[sent], in_s.at[a])
        for a in range(2):
            arrived(qb, fw_s.at[a])
            arrived(st.at[a], ex_s.at[a])
        arrived(c_st, c1_s)
        arrived(hida.at[pl.ds(1, 7)], hid_s)
        arrived(cga.at[pl.ds(1, 7)], cg_s)
        for a in range(3):
            arrived(qb.at[sent], out_s.at[a])
    with jax.named_scope("drain_weight"):
        arrived(w_o.at[pl.ds(0, 3)], w_s)
        arrived(w_o, w_r)
    with jax.named_scope("drain_key"):
        arrived(dk_o.at[0], out_r.at[1])
    with jax.named_scope("drain_value"):
        arrived(dv_o.at[0], out_r.at[2])
    with jax.named_scope("drain_query"):
        arrived(dq_o.at[0], out_r.at[0])


def place(dq, dk, dv, parts, dq_o, dk_o, dv_o, w_o, held, held_w, full_w, in_s, out_s, w_s):
    fetch_w = pltpu.make_async_copy(parts, held_w, w_s.at[0])
    store_w = pltpu.make_async_copy(full_w, w_o, w_s.at[1])
    fetches = [
        pltpu.make_async_copy(src, held.at[a], in_s.at[a]) for a, src in enumerate((dq, dk, dv))
    ]
    stores = [
        pltpu.make_async_copy(held.at[a], dst, out_s.at[a])
        for a, dst in enumerate((dq_o, dk_o, dv_o))
    ]
    fetch_w.start()
    for fetch in fetches:
        fetch.start()
    fetch_w.wait()
    for half in range(2):
        for array in range(2):
            columns = slice(half * HD, (half + 1) * HD)
            full_w[:, array, columns] = held_w[2 * half + array].astype(F32)
    store_w.start()
    for fetch, store in zip(fetches, stores):
        fetch.wait()
        store.start()
    store_w.wait()
    for store in stores:
        store.wait()


def on_device(latent_query, latent_key, latent_value, out_grad, query_hidden, cond_weight):
    anywhere = pl.BlockSpec(memory_space=pl.ANY)
    token = jax.ShapeDtypeStruct(latent_query.shape, BF16)
    dma = pltpu.SemaphoreType.DMA
    total_keys = KEYS + COND
    grads = pl.pallas_call(
        kernel,
        name="attention_backward",
        out_shape=(token, token, token, jax.ShapeDtypeStruct((4, 112, HD), BF16)),
        in_specs=[anywhere] * 6,
        out_specs=(anywhere,) * 4,
        scratch_shapes=[
            pltpu.VMEM((SLOTS * ROWS, HD), BF16),
            pltpu.VMEM((SLOTS * ROWS, HD), BF16),
            pltpu.VMEM((total_keys, HD), BF16),
            pltpu.VMEM((total_keys, HD), BF16),
            *(pltpu.VMEM((2 * HD, n), BF16) for n in QB),
            *(pltpu.VMEM((HD, n), BF16) for n in QB * 3),
            *(pltpu.VMEM((total_keys, n), BF16) for n in QB),
            pltpu.VMEM((total_keys, QB[0]), F32),
            pltpu.VMEM(((BACK_TILES - KEPT) * BT, QB[1]), F32),
            *(pltpu.VMEM((16, n), F32) for n in QB),
            pltpu.VMEM((total_keys, HD), F32),
            pltpu.VMEM((total_keys, HD), F32),
            *(pltpu.VMEM((HD, n), F32) for n in QB),
            pltpu.VMEM((2, SLOTS, ROWS, HD), BF16),
            pltpu.VMEM((2, SLOTS, ROWS, HD), BF16),
            pltpu.VMEM((cond_weight.shape[0], 2, HD), BF16),
            pltpu.VMEM(query_hidden.shape, BF16),
            pltpu.VMEM((8, COND, WINDOW), BF16),
            pltpu.VMEM((COND, HD), BF16),
            pltpu.VMEM((COND, HD), BF16),
            pltpu.VMEM((8, COND, HD), BF16),
            pltpu.VMEM((WINDOW, HD), BF16),
            dma((4,)), dma((2, 2)), dma((TILES,)),
            dma((2,)), dma((TILES,)),
            dma((2,)), dma((2, BACK_TILES + 1)),
            dma((3,)), dma((3,)),
            dma, dma,
            dma, dma,
            dma, dma,
            dma, dma,
            dma, dma,
        ],
        compiler_params=pltpu.CompilerParams(
            collective_id=0, has_side_effects=True, vmem_limit_bytes=63 << 20
        ),
    )(latent_query, latent_key, latent_value, out_grad, query_hidden, cond_weight)
    weight = jax.ShapeDtypeStruct((112, 2, 2 * HD), F32)
    return pl.pallas_call(
        place,
        name="place_outputs",
        out_shape=(token, token, token, weight),
        in_specs=[anywhere] * 4,
        out_specs=(anywhere,) * 4,
        scratch_shapes=[
            pltpu.VMEM((3,) + latent_query.shape, BF16),
            pltpu.VMEM((4, 112, HD), BF16),
            pltpu.VMEM((112, 2, 2 * HD), F32),
            dma((3,)), dma((3,)), dma((2,)),
        ],
    )(*grads)


def solution(mesh):
    placed = (
        P("dp", ("seq", "tp"), None),
        P("dp", ("seq", "tp"), None),
        P("dp", ("seq", "tp"), None),
        P("dp", ("seq", "tp"), None),
        P("dp", None, None),
        P(None, None, "seq"),
    )
    return jax.shard_map(
        on_device,
        mesh=mesh,
        in_specs=placed,
        out_specs=(
            P("dp", ("seq", "tp"), None),
            P("dp", ("seq", "tp"), None),
            P("dp", ("seq", "tp"), None),
            P(("dp", "tp"), None, "seq"),
        ),
        check_vma=False,
    )
```
